512 devices in a mesh: blk: 32 (over x_hi, y, core), grp: 16 (over z, x_lo).
Axes of the slice: x: 4 (x_hi: 2, x_lo: 2; x = x_hi * 2 + x_lo), y: 8, z: 8, core: 2. Of those that a mesh axis runs over, the one named last changes fastest.
Arguments:
- users: float32 [65536, 256], P(('blk', 'grp'))
- items: float32 [16384, 256], P(('blk', 'grp'))
- counts: int32 [16384], P(('blk', 'grp')), may hold values from 50 to 15000
- target_indices: int32 [65536], P(('blk', 'grp')), may hold values from 0 to 16383, as said below
Outputs:
- loss: float32 [], replicated
- query_tower_slope: float32 [65536, 256], P(('blk', 'grp'))
- candidate_tower_slope: float32 [16384, 256], P(('blk', 'grp'))
The draws below stay inside these ranges and needn't reach their ends.
Inputs may be any that keep to these rules, and one draw needn't show every extreme that they name: `target_indices`: user rows of the k-th aligned block of 128 rows name items of the k-th aligned block of 32 items, each such item named by exactly 4 of them.
All inputs are finite; a program needn't handle non-finite values.
Results may differ from the reference program's by a relative error of at most 0.012.
The reference program's roundings to bfloat16 on the way count: a program that leaves them out, or rounds other values in their place, can miss the bound.
Values may be sent and summed in bfloat16 or wider, within the bound.
A program may use at most 64 MiB of HBM per device.

```python
import math
import jax
import jax.numpy as jnp
from jax import lax

D = 256
USERS_DEV = 128
ITEMS_DEV = 32
USERS = 65536
ITEMS = 16384


def shared_items(key):
    return jax.random.normal(jax.random.fold_in(key, 101), (ITEMS, D), jnp.float32)


def shared_counts(key):
    sub = jax.random.fold_in(key, 202)
    base = jax.random.randint(sub, (ITEMS,), 50, 320)
    region_mult = jax.random.randint(jax.random.fold_in(key, 212), (4,), 1, 16)
    item_rank = jnp.arange(ITEMS, dtype=jnp.int32)
    region = item_rank * 4 // ITEMS
    multiplier = region_mult[region]
    ramp = 100 + 200 * item_rank // ITEMS
    values = jnp.minimum(base * multiplier * ramp // 100, 15000)
    top_position = jax.random.randint(jax.random.fold_in(key, 222), (), 0, ITEMS)
    return jnp.where(item_rank == top_position, 15000, values).astype(jnp.int32)


def shared_targets(key):
    key = jax.random.fold_in(key, 303)
    blocks = USERS // USERS_DEV
    keys = jax.random.split(key, blocks)
    perms = jax.vmap(lambda sub: jax.random.permutation(sub, USERS_DEV))(keys)
    offsets = jnp.arange(blocks, dtype=jnp.int32)[:, None] * ITEMS_DEV
    return (perms.astype(jnp.int32) % ITEMS_DEV + offsets).reshape(USERS)


def draw_items(key, part):
    return shared_items(key)


def draw_counts(key, part):
    return shared_counts(key)


def draw_target_indices(key, part):
    return shared_targets(key)


def draw_users(key, part):
    item_rows = shared_items(key)
    target_rows = shared_targets(key)
    key = jax.random.fold_in(key, 3)
    rowid = jnp.arange(USERS, dtype=jnp.int32)
    region_alpha = jax.random.uniform(jax.random.fold_in(key, 9), (4,), jnp.float32, 0.05, 0.25)
    alpha = region_alpha[rowid * 4 // USERS]
    leaning = alpha[:, None] * item_rows[target_rows]
    return jax.random.normal(key, (USERS, D), jnp.float32) + leaning


def setup_inputs(seed: int = 0) -> dict:
    seeds = jax.random.split(jax.random.key(seed), 5)
    return {
        "users": draw_users(jax.random.fold_in(seeds[4], 71), 0),
        "items": draw_items(jax.random.fold_in(seeds[4], 71), 0),
        "counts": draw_counts(jax.random.fold_in(seeds[4], 71), 0),
        "target_indices": draw_target_indices(jax.random.fold_in(seeds[4], 71), 0),
    }


scaling_divisor = 5.0


def reference(users, items, counts, target_indices):
    user_half = users.astype(jnp.bfloat16)
    candidate_midpoint = items.astype(jnp.bfloat16)
    logq_half = lax.optimization_barrier(jnp.log(counts.astype(jnp.float32)).astype(jnp.bfloat16))
    draw_chance_logarithm = logq_half.astype(jnp.float32)
    block = math.gcd(USERS, 1024)
    user_blocks = user_half.reshape(USERS // block, block, D)

    def visit(item_total, query_vectors):
        score_table = jnp.dot(query_vectors, candidate_midpoint.T, preferred_element_type=jnp.float32) / scaling_divisor - draw_chance_logarithm[None, :]
        top = jnp.max(score_table, axis=1)
        lse = top + jnp.log(jnp.sum(jnp.exp(score_table - top[:, None]), axis=1))
        weights = jnp.exp(score_table - lse[:, None]).astype(jnp.bfloat16)
        user_part = jnp.dot(weights, candidate_midpoint, preferred_element_type=jnp.float32)
        item_total = item_total + jnp.dot(weights.T, query_vectors, preferred_element_type=jnp.float32)
        return item_total, (lse, user_part)

    candidate_accumulator, (lse, query_accumulator) = lax.scan(visit, jnp.zeros((ITEMS, D), jnp.float32), user_blocks)
    lse = lse.reshape(USERS)
    query_accumulator = query_accumulator.reshape(USERS, D)
    query_whole = user_half.astype(jnp.float32)
    item_full = candidate_midpoint.astype(jnp.float32)
    target_candidate_vectors = item_full[target_indices]
    target_score = jnp.sum(query_whole * target_candidate_vectors, axis=1) / scaling_divisor - draw_chance_logarithm[target_indices]
    loss = jnp.sum(lse - target_score) / USERS
    query_tower_slope = (query_accumulator - target_candidate_vectors) / scaling_divisor
    target_query_vectors = jnp.zeros((ITEMS, D), jnp.float32).at[target_indices].add(query_whole)
    candidate_tower_slope = (candidate_accumulator - target_query_vectors) / scaling_divisor
    return loss, query_tower_slope, candidate_tower_slope
```

```python
import functools
import math

import jax
import jax.numpy as jnp
from jax import lax
from jax.experimental import pallas as pl
from jax.experimental.pallas import tpu as pltpu
from jax.sharding import PartitionSpec as P

scaling_divisor = 5.0
LOG2E = math.log2(math.e)
LN2 = math.log(2.0)
MESH = pl.DeviceIdType.MESH
BF16 = jnp.bfloat16
F32 = jnp.float32

NX, NY, NZ = 4, 8, 8
UD, ID, D = 128, 32, 256
ORDER = (0, 1, 7, 2, 6, 3, 5, 4)
SLOT = tuple(ORDER.index(k) for k in range(NY))
HALF = NX * NY * ID // 2


def offset_of(k):
    return jnp.where(k % 2 == 1, (k + 1) // 2, (8 - k // 2) % 8)


def dot(a, b, ca=1, cb=0):
    return lax.dot_general(a, b, (((ca,), (cb,)), ((), ())), preferred_element_type=F32)


def kernel(
    users_ref, items_ref, counts_ref, tgt_ref,
    loss_ref, query_ref, cand_ref,
    rows, it, lq, it_t, lqc, p_all, acc, mst, lst, st_out, st_in, pt_out, pt_in,
    w_row, own_f, ip, xc_in, xs_in, ys_out, ys_in, loss_out, loss_in, tq_s, tv_s,
    z_ss, z_rs, y_ss, y_rs, ql_ss, ql_rs, x_ss, x_rs, qx_ss, qx_rs, c_ss, c_rs,
    st_ss, st_rs, pt_ss, pt_rs, xc_ss, xc_rs, xs_ss, xs_rs, ys_ss, ys_rs, ls_ss, ls_rs,
):
    b = lax.axis_index("blk")
    g = lax.axis_index("grp")
    x = (b // 16) * 2 + g % 2
    y = (b // 2) % 8
    z = g // 2
    core = b % 2

    def device(dx=0, dy=0, dz=0, dc=0):
        xx = (x + dx) % NX
        return (
            ((xx // 2) * 8 + (y + dy) % NY) * 2 + (core + dc) % 2,
            ((z + dz) % NZ) * 2 + xx % 2,
        )

    def copy(src, dst, ss, rs, **to):
        return pltpu.make_async_remote_copy(
            src_ref=src, dst_ref=dst, send_sem=ss, recv_sem=rs,
            device_id=device(**to), device_id_type=MESH,
        )

    barrier = pltpu.get_barrier_semaphore()
    for d in range(1, NZ):
        pl.semaphore_signal(barrier, inc=1, device_id=device(dz=d), device_id_type=MESH)
    for d in range(1, NY):
        pl.semaphore_signal(barrier, inc=1, device_id=device(dy=d), device_id_type=MESH)
    for d in range(1, NX):
        pl.semaphore_signal(barrier, inc=1, device_id=device(dx=d), device_id_type=MESH)
    pl.semaphore_signal(barrier, inc=1, device_id=device(dc=1), device_id_type=MESH)

    rows[0] = users_ref[...].astype(BF16)
    it[0, 0:ID, :] = items_ref[...].astype(BF16)
    logq = jnp.log(counts_ref[...].astype(F32)).astype(BF16).astype(F32)
    logq = jnp.concatenate([logq, jnp.zeros((1, 128 - ID), F32)], axis=1)
    lq[0, 0, 0] = logq

    pl.semaphore_wait(barrier, NZ + NY + NX - 3 + 1)

    def z_copy(d):
        return copy(rows.at[0], rows.at[(NZ - d) % NZ], z_ss.at[d], z_rs.at[(NZ - d) % NZ], dz=d)

    def y_copy(d):
        s = SLOT[(NY - d) % NY]
        return copy(
            it.at[0, pl.ds(0, ID)], it.at[0, pl.ds(s * NX * ID, ID)], y_ss.at[d], y_rs.at[s], dy=d
        )

    def ql_copy(d):
        s = SLOT[(NY - d) % NY]
        return copy(lq.at[0, 0, 0], lq.at[0, s, 0], ql_ss.at[d], ql_rs.at[s], dy=d)

    def x_copy(s, e):
        return copy(
            it.at[0, pl.ds(s * NX * ID, ID)],
            it.at[0, pl.ds((s * NX + NX - e) * ID, ID)],
            x_ss.at[s, e], x_rs.at[s, NX - e], dx=e,
        )

    def qx_copy(e):
        return copy(lq.at[0, :, 0], lq.at[0, :, NX - e], qx_ss.at[e], qx_rs.at[NX - e], dx=e)

    def c_copy(h):
        part = pl.ds(h * HALF, HALF)
        return copy(it.at[0, part], it.at[1, part], c_ss.at[h], c_rs.at[h], dc=1)

    def qc_copy():
        return copy(lq.at[0], lq.at[1], c_ss.at[2], c_rs.at[2], dc=1)

    for d in ORDER[1:]:
        ql_copy(d).start()
        y_copy(d).start()
        z_copy(d).start()
    for e in range(1, NX):
        x_copy(0, e).start()

    first = (b * 16 + g) * ID
    hot = (
        lax.broadcasted_iota(jnp.int32, (ID, UD), 0) + first == tgt_ref[...]
    ).astype(F32)
    hot_half = hot.astype(BF16)
    own_items = it[0, 0:ID, :]
    tq = dot(hot_half, rows[0])
    tq_s[...] = tq
    tv_s[...] = dot(own_items, hot_half, 0, 0)
    eye = (
        lax.broadcasted_iota(jnp.int32, (ID, 128), 0)
        == lax.broadcasted_iota(jnp.int32, (ID, 128), 1)
    )
    own_logq = jnp.where(eye, jnp.broadcast_to(logq, (ID, 128)), 0.0)
    named = jnp.sum(hot, axis=1, keepdims=True)
    pos = jnp.sum(
        jnp.sum(tq * own_items.astype(F32), axis=1, keepdims=True) * (1.0 / scaling_divisor)
        - jnp.sum(own_logq, axis=1, keepdims=True) * named,
        axis=0, keepdims=True,
    )
    st_out[1] = jnp.broadcast_to(pos, (8, 128))

    def forward(s, carry):
        pltpu.make_async_copy(
            it.at[0, pl.ds(0, ID)], it.at[0, pl.ds(s * NX * ID, ID)], y_rs.at[s]
        ).wait()
        for e in range(1, NX):
            x_copy(s, e).start()
        return carry

    lax.fori_loop(1, 4, forward, 0)
    for s in range(1, NY):
        pltpu.make_async_copy(lq.at[0, 0, 0], lq.at[0, s, 0], ql_rs.at[s]).wait()
    for e in range(1, NX):
        qx_copy(e).start()
    lax.fori_loop(4, 8, forward, 0)
    for e in range(1, NX):
        pltpu.make_async_copy(lq.at[0, :, 0], lq.at[0, :, e], qx_rs.at[e]).wait()
    qc_copy().start()

    def arrived(s, carry):
        for e in range(1, NX):
            spot = it.at[0, pl.ds((s * NX + e) * ID, ID)]
            pltpu.make_async_copy(spot, spot, x_rs.at[s, e]).wait()
        return carry

    ones = jnp.ones((128, 128), BF16)

    def prepare(blk):
        side, half = blk // 2, blk % 2
        it_t[blk] = it[side, half * HALF : (half + 1) * HALF, :].T

        def column(i, carry):
            row = jnp.broadcast_to(lq[side, half * 4 + i // 4, i % 4], (ID, 128))
            spread = jnp.where(eye, row, 0.0).astype(BF16)
            lqc[blk, pl.ds(pl.multiple_of(i * ID, ID), ID), :] = dot(spread, ones) * LOG2E
            return carry

        lax.fori_loop(0, 16, column, 0)

    def unit(blk, s):
        side, half = blk // 2, blk % 2
        scores = dot(
            it[side, pl.ds(pl.multiple_of(half * HALF, HALF), HALF), :], rows[s], 1, 1
        )
        t = scores * (LOG2E / scaling_divisor) - lqc[blk]
        m = jnp.max(t, axis=0, keepdims=True)
        p = jnp.exp2(t - m)
        mst[blk, pl.ds(s, 1), :] = m
        lst[blk, pl.ds(s, 1), :] = jnp.sum(p, axis=0, keepdims=True)
        p = p.astype(BF16)
        p_all[blk, :, pl.ds(pl.multiple_of(s * UD, UD), UD)] = p
        acc[blk, s] = dot(it_t[blk], p)

    def wait_users(k):
        s = offset_of(k)
        pltpu.make_async_copy(rows.at[0], rows.at[s], z_rs.at[s]).wait()

    def early(blk):
        def step(k, carry):
            unit(blk, offset_of(k))
            return carry

        lax.fori_loop(0, 3, step, 0)

    lax.fori_loop(0, 4, arrived, 0)
    c_copy(0).start()
    prepare(0)
    wait_users(1)
    wait_users(2)
    early(0)
    lax.fori_loop(4, 8, arrived, 0)
    c_copy(1).start()
    prepare(1)
    early(1)
    qc_copy().wait_recv()
    c_copy(0).wait_recv()
    prepare(2)
    early(2)
    c_copy(1).wait_recv()
    prepare(3)
    early(3)

    def late(k, carry):
        wait_users(k)

        def step(blk, carry):
            unit(blk, offset_of(k))
            return carry

        return lax.fori_loop(0, 4, step, carry)

    lax.fori_loop(3, 8, late, 0)

    top = jnp.max(mst[...], axis=0)
    local = top + jnp.log2(sum(lst[k] * jnp.exp2(mst[k] - top) for k in range(4)))
    st_out[0] = local

    def st_copy(d):
        return copy(st_out, st_in.at[(NZ - d) % NZ], st_ss.at[d], st_rs.at[(NZ - d) % NZ], dz=d)

    def pt_copy(d):
        return copy(
            pt_out.at[d], pt_in.at[(NZ - d) % NZ], pt_ss.at[d], pt_rs.at[(NZ - d) % NZ], dz=d
        )

    for d in (4, 3, 5, 2, 6, 1, 7):
        st_copy(d).start()

    for k in range(4):
        lst[k] = jnp.exp2(mst[k] - local)

    def part_of(s):
        return sum(acc[k, s] * lst[k, pl.ds(s, 1), :] for k in range(4))

    def give(s, carry):
        pt_out[s] = part_of(s).astype(BF16)
        pt_copy(s).start()
        return carry

    lax.fori_loop(1, NZ, give, 0)

    for e in range(1, NZ):
        pltpu.make_async_copy(st_out, st_in.at[e], st_rs.at[e]).wait()
    seen = [local] + [jnp.roll(st_in[e, 0], e, axis=0) for e in range(1, NZ)]
    top = functools.reduce(jnp.maximum, seen)
    lse = top + jnp.log2(sum(jnp.exp2(v - top) for v in seen))
    share = [jnp.exp2(v[0:1] - lse[0:1]) for v in seen]
    for k in range(4):
        w = jnp.exp2(mst[k] - lse).astype(BF16)
        for s in range(NZ):
            w_row[k, :, s * UD : (s + 1) * UD] = w[s : s + 1, :]

    def item_part(blk, c):
        chunk = pl.ds(pl.multiple_of(c * 128, 128), 128)
        weights = p_all[blk, chunk, :] * w_row[blk]
        return dot(weights, rows[...].reshape(NZ * UD, D))

    def xc_copy(h):
        part = pl.ds(h * HALF, HALF)
        return copy(ip.at[1, part], xc_in.at[part], xc_ss.at[h], xc_rs.at[h], dc=1)

    for h in (1, 0):
        def other(c, carry):
            spot = pl.ds(pl.multiple_of(h * HALF + c * 128, 128), 128)
            ip[1, spot, :] = item_part(2 + h, c).astype(BF16)
            return carry

        lax.fori_loop(0, 4, other, 0)
        xc_copy(h).start()

    for h in (1, 0):
        def own(c, carry):
            spot = pl.ds(pl.multiple_of(h * HALF + c * 128, 128), 128)
            own_f[spot, :] = item_part(h, c)
            return carry

        lax.fori_loop(0, 4, own, 0)

    def ls_copy(i, j, **to):
        return copy(loss_out.at[i], loss_in.at[j], ls_ss.at[j], ls_rs.at[j], **to)

    pos_all = st_out[1] + sum(st_in[e, 1] for e in range(1, NZ))
    line = jnp.sum(jnp.sum(lse, axis=1, keepdims=True), axis=0, keepdims=True) * LN2
    loss_out[0] = jnp.broadcast_to(line, (8, 128)) - pos_all
    ls_copy(0, 0, dc=1).start()

    def xs_copy(s, e):
        return copy(
            ip.at[0, pl.ds((s * NX + e) * ID, ID)], xs_in.at[s, NX - e],
            xs_ss.at[s, e], xs_rs.at[s, NX - e], dx=e,
        )

    for h in (1, 0):
        xc_copy(h).wait_recv()

        def own_sum(s, carry):
            spot = pl.ds(pl.multiple_of(s * NX * ID, NX * ID), NX * ID)
            total = own_f[spot, :] + xc_in[spot, :].astype(F32)
            own_f[spot, :] = total
            ip[0, spot, :] = total.astype(BF16)
            for e in (2, 1, 3):
                xs_copy(s, e).start()
            return carry

        lax.fori_loop(h * 4, h * 4 + 4, own_sum, 0)

    ls_copy(0, 0, dc=1).wait_recv()
    loss_out[1] = loss_out[0] + loss_in[0]
    for e in range(1, NX):
        ls_copy(1, e, dx=e).start()

    def ys_copy(s):
        o = offset_of(s)
        mirror = jnp.where(s == 0, 0, jnp.where(s == 7, 7, jnp.where(s % 2 == 1, s + 1, s - 1)))
        return copy(ys_out.at[s], ys_in.at[mirror], ys_ss.at[s], ys_rs.at[mirror], dy=o)

    def x_total(s):
        for e in range(1, NX):
            pltpu.make_async_copy(xs_in.at[s, e], xs_in.at[s, e], xs_rs.at[s, e]).wait()
        spot = pl.ds(pl.multiple_of(s * NX * ID, NX * ID), ID)
        return own_f[spot, :] + sum(xs_in[s, e].astype(F32) for e in range(1, NX))

    def relay(i, carry):
        s = 7 - i
        ys_out[s] = x_total(s).astype(BF16)
        ys_copy(s).start()
        return carry

    lax.fori_loop(0, 7, relay, 0)
    for e in range(1, NX):
        ls_copy(1, e, dx=e).wait_recv()
    loss_out[2] = loss_out[1] + loss_in[1] + loss_in[2] + loss_in[3]
    for d in range(1, NY):
        ls_copy(2, 3 + d, dy=d).start()
    cand = x_total(0) - tq_s[...]

    user_sum = part_of(0) * share[0] - tv_s[...]
    for e in range(1, NZ):
        pltpu.make_async_copy(pt_in.at[e], pt_in.at[e], pt_rs.at[e]).wait()
        user_sum = user_sum + pt_in[e].astype(F32) * share[e]
    query_ref[...] = user_sum.T * (1.0 / scaling_divisor)

    for s in range(1, NY):
        pltpu.make_async_copy(ys_in.at[s], ys_in.at[s], ys_rs.at[s]).wait()
        cand = cand + ys_in[s].astype(F32)
    cand_ref[...] = cand * (1.0 / scaling_divisor)
    total = loss_out[2]
    for d in range(1, NY):
        ls_copy(2, 3 + d, dy=d).wait_recv()
        total = total + loss_in[3 + d]
    users_all = 2 * NX * NY * NZ * UD
    loss_ref[...] = total[0:1, 0:1] * (1.0 / users_all)

    for d in range(1, NZ):
        z_copy(d).wait_send()
        y_copy(d).wait_send()
        ql_copy(d).wait_send()
        st_copy(d).wait_send()
        pt_copy(d).wait_send()
        ls_copy(2, 3 + d, dy=d).wait_send()
    for e in range(1, NX):
        qx_copy(e).wait_send()
        ls_copy(1, e, dx=e).wait_send()

    def left(s, carry):
        for e in range(1, NX):
            x_copy(s, e).wait_send()
            xs_copy(s, e).wait_send()
        return carry

    lax.fori_loop(0, NY, left, 0)

    def left_y(s, carry):
        ys_copy(s).wait_send()
        return carry

    lax.fori_loop(1, NY, left_y, 0)
    for h in range(2):
        c_copy(h).wait_send()
        xc_copy(h).wait_send()
    qc_copy().wait_send()
    ls_copy(0, 0, dc=1).wait_send()


def on_device(users, items, counts, target_indices):
    dma = lambda *n: pltpu.SemaphoreType.DMA(n)
    pair = lambda *n: [dma(*n), dma(*n)]
    vmem = pl.BlockSpec(memory_space=pltpu.VMEM)
    loss, query, cand = pl.pallas_call(
        kernel,
        out_shape=(
            jax.ShapeDtypeStruct((1, 1), F32),
            jax.ShapeDtypeStruct((UD, D), F32),
            jax.ShapeDtypeStruct((ID, D), F32),
        ),
        in_specs=[vmem] * 4,
        out_specs=(vmem,) * 3,
        scratch_shapes=[
            pltpu.VMEM((NZ, UD, D), BF16),
            pltpu.VMEM((2, 2 * HALF, D), BF16),
            pltpu.VMEM((2, NY, NX, 1, 128), F32),
            pltpu.VMEM((4, D, HALF), BF16),
            pltpu.VMEM((4, HALF, 128), F32),
            pltpu.VMEM((4, HALF, NZ * UD), BF16),
            pltpu.VMEM((4, NZ, D, UD), F32),
            pltpu.VMEM((4, NZ, UD), F32),
            pltpu.VMEM((4, NZ, UD), F32),
            pltpu.VMEM((2, 8, 128), F32),
            pltpu.VMEM((NZ, 2, 8, 128), F32),
            pltpu.VMEM((NZ, D, UD), BF16),
            pltpu.VMEM((NZ, D, UD), BF16),
            pltpu.VMEM((4, 1, NZ * UD), BF16),
            pltpu.VMEM((2 * HALF, D), F32),
            pltpu.VMEM((2, 2 * HALF, D), BF16),
            pltpu.VMEM((2 * HALF, D), BF16),
            pltpu.VMEM((NY, NX, ID, D), BF16),
            pltpu.VMEM((NY, ID, D), BF16),
            pltpu.VMEM((NY, ID, D), BF16),
            pltpu.VMEM((3, 8, 128), F32),
            pltpu.VMEM((11, 8, 128), F32),
            pltpu.VMEM((ID, D), F32),
            pltpu.VMEM((D, UD), F32),
            *pair(NZ), *pair(NY), *pair(NY), *pair(NY, NX), *pair(NX), *pair(3),
            *pair(NZ), *pair(NZ), *pair(2), *pair(NY, NX), *pair(NY), *pair(11),
        ],
        compiler_params=pltpu.CompilerParams(
            collective_id=0, has_side_effects=True, vmem_limit_bytes=48 * 2**20
        ),
        cost_estimate=pl.CostEstimate(
            flops=6 * 1024 * 2048 * D, bytes_accessed=2**19, transcendentals=1024 * 2048
        ),
        name="towers",
    )(users, items, counts.reshape(1, ID), target_indices.reshape(1, UD))
    return loss.reshape(()), query, cand


def solution(mesh):
    placed = P(("blk", "grp"))
    wide = P(("blk", "grp"), None)
    return jax.shard_map(
        on_device,
        mesh=mesh,
        in_specs=(wide, wide, placed, placed),
        out_specs=(P(), wide, wide),
        check_vma=False,
    )
```

```python
import functools
import math

import jax
import jax.numpy as jnp
from jax import lax
from jax.experimental import pallas as pl
from jax.experimental.pallas import tpu as pltpu
from jax.sharding import PartitionSpec as P

scaling_divisor = 5.0
LOG2E = math.log2(math.e)
LN2 = math.log(2.0)
MESH = pl.DeviceIdType.MESH
BF16 = jnp.bfloat16
F32 = jnp.float32

NX, NY, NZ = 4, 8, 8
UD, ID, D = 128, 32, 256
ORDER = (0, 1, 7, 2, 6, 3, 5, 4)
SLOT = tuple(ORDER.index(k) for k in range(NY))
HALF = NX * NY * ID // 2


def offset_of(k):
    return jnp.where(k % 2 == 1, (k + 1) // 2, (8 - k // 2) % 8)


def dot(a, b, ca=1, cb=0):
    return lax.dot_general(a, b, (((ca,), (cb,)), ((), ())), preferred_element_type=F32)


def kernel(
    users_hbm, items_hbm, counts_hbm, tgt_hbm,
    loss_ref, query_ref, cand_ref,
    users_ref, items_ref, counts_ref, tgt_ref, in_sem,
    rows, it, lq, it_t, lqc, p_all, acc, mst, lst, st_out, st_in, pt_out, pt_in,
    w_row, own_f, ip, xc_in, xs_in, ys_out, ys_in, loss_out, loss_in, tq_s, tv_s,
    z_ss, z_rs, y_ss, y_rs, ql_ss, ql_rs, x_ss, x_rs, qx_ss, qx_rs, c_ss, c_rs,
    st_ss, st_rs, pt_ss, pt_rs, xc_ss, xc_rs, xs_ss, xs_rs, ys_ss, ys_rs, ls_ss, ls_rs,
):
    b = lax.axis_index("blk")
    g = lax.axis_index("grp")
    x = (b // 16) * 2 + g % 2
    y = (b // 2) % 8
    z = g // 2
    core = b % 2

    def device(dx=0, dy=0, dz=0, dc=0):
        xx = (x + dx) % NX
        return (
            ((xx // 2) * 8 + (y + dy) % NY) * 2 + (core + dc) % 2,
            ((z + dz) % NZ) * 2 + xx % 2,
        )

    def copy(src, dst, ss, rs, **to):
        return pltpu.make_async_remote_copy(
            src_ref=src, dst_ref=dst, send_sem=ss, recv_sem=rs,
            device_id=device(**to), device_id_type=MESH,
        )

    barrier = pltpu.get_barrier_semaphore()
    for d in range(1, NZ):
        pl.semaphore_signal(barrier, inc=1, device_id=device(dz=d), device_id_type=MESH)
    for d in range(1, NY):
        pl.semaphore_signal(barrier, inc=1, device_id=device(dy=d), device_id_type=MESH)
    for d in range(1, NX):
        pl.semaphore_signal(barrier, inc=1, device_id=device(dx=d), device_id_type=MESH)
    pl.semaphore_signal(barrier, inc=1, device_id=device(dc=1), device_id_type=MESH)

    loads = [
        pltpu.make_async_copy(src, dst, in_sem.at[k])
        for k, (src, dst) in enumerate((
            (counts_hbm, counts_ref), (items_hbm, items_ref), (users_hbm, users_ref), (tgt_hbm, tgt_ref)
        ))
    ]
    for load in loads:
        load.start()
    for load in loads:
        load.wait()
    rows[0] = users_ref[...].astype(BF16)
    it[0, 0:ID, :] = items_ref[...].astype(BF16)
    logq = jnp.log(counts_ref[...].astype(F32)).astype(BF16).astype(F32)
    logq = jnp.concatenate([logq, jnp.zeros((1, 128 - ID), F32)], axis=1)
    lq[0, 0, 0] = logq

    pl.semaphore_wait(barrier, NZ + NY + NX - 3 + 1)

    def z_copy(d):
        s = SLOT[(NZ - d) % NZ]
        return copy(rows.at[0], rows.at[s], z_ss.at[d], z_rs.at[s], dz=d)

    def y_copy(d):
        s = SLOT[(NY - d) % NY]
        return copy(
            it.at[0, pl.ds(0, ID)], it.at[0, pl.ds(s * NX * ID, ID)], y_ss.at[d], y_rs.at[s], dy=d
        )

    def ql_copy(d):
        s = SLOT[(NY - d) % NY]
        return copy(lq.at[0, 0, 0], lq.at[0, s, 0], ql_ss.at[d], ql_rs.at[s], dy=d)

    def x_copy(s, e):
        return copy(
            it.at[0, pl.ds(s * NX * ID, ID)],
            it.at[0, pl.ds((s * NX + NX - e) * ID, ID)],
            x_ss.at[s, e], x_rs.at[s, NX - e], dx=e,
        )

    def qx_copy(e):
        return copy(lq.at[0, :, 0], lq.at[0, :, NX - e], qx_ss.at[e], qx_rs.at[NX - e], dx=e)

    def c_copy(h):
        part = pl.ds(h * HALF, HALF)
        return copy(it.at[0, part], it.at[1, part], c_ss.at[h], c_rs.at[h], dc=1)

    def qc_copy():
        return copy(lq.at[0], lq.at[1], c_ss.at[2], c_rs.at[2], dc=1)

    for d in ORDER[1:]:
        ql_copy(d).start()
        y_copy(d).start()
        z_copy(d).start()
    for e in range(1, NX):
        x_copy(0, e).start()

    first = (b * 16 + g) * ID
    hot = (
        lax.broadcasted_iota(jnp.int32, (ID, UD), 0) + first == tgt_ref[...]
    ).astype(F32)
    hot_half = hot.astype(BF16)
    own_items = it[0, 0:ID, :]
    tq = dot(hot_half, rows[0])
    tq_s[...] = tq
    tv_s[...] = dot(own_items, hot_half, 0, 0)
    eye = (
        lax.broadcasted_iota(jnp.int32, (ID, 128), 0)
        == lax.broadcasted_iota(jnp.int32, (ID, 128), 1)
    )
    own_logq = jnp.where(eye, jnp.broadcast_to(logq, (ID, 128)), 0.0)
    named = jnp.sum(hot, axis=1, keepdims=True)
    pos = jnp.sum(
        jnp.sum(tq * own_items.astype(F32), axis=1, keepdims=True) * (1.0 / scaling_divisor)
        - jnp.sum(own_logq, axis=1, keepdims=True) * named,
        axis=0, keepdims=True,
    )
    st_out[1] = jnp.broadcast_to(pos, (8, 128))

    def forward(s, carry):
        pltpu.make_async_copy(
            it.at[0, pl.ds(0, ID)], it.at[0, pl.ds(s * NX * ID, ID)], y_rs.at[s]
        ).wait()
        for e in range(1, NX):
            x_copy(s, e).start()
        return carry

    lax.fori_loop(1, 4, forward, 0)
    for s in range(1, NY):
        pltpu.make_async_copy(lq.at[0, 0, 0], lq.at[0, s, 0], ql_rs.at[s]).wait()
    for e in range(1, NX):
        qx_copy(e).start()
    lax.fori_loop(4, 8, forward, 0)
    for e in range(1, NX):
        pltpu.make_async_copy(lq.at[0, :, 0], lq.at[0, :, e], qx_rs.at[e]).wait()
    qc_copy().start()

    def arrived(s, carry):
        for e in range(1, NX):
            spot = it.at[0, pl.ds((s * NX + e) * ID, ID)]
            pltpu.make_async_copy(spot, spot, x_rs.at[s, e]).wait()
        return carry

    ones = jnp.ones((128, 128), BF16)

    def prepare(blk):
        side, half = blk // 2, blk % 2
        it_t[blk] = it[side, half * HALF : (half + 1) * HALF, :].T
        row = lq[side, half * 4 : (half + 1) * 4].reshape(16, 1, 128)
        spread = jnp.where(eye[None], jnp.broadcast_to(row, (16, ID, 128)), 0.0)
        lqc[blk] = dot(spread.reshape(HALF, 128).astype(BF16), ones) * LOG2E

    def unit(blk, k):
        side, half = blk // 2, blk % 2
        pair = rows[2 * k : 2 * k + 2].reshape(2 * UD, D)
        scores = dot(it[side, half * HALF : (half + 1) * HALF, :], pair, 1, 1)
        lift = lqc[blk]
        t = scores * (LOG2E / scaling_divisor) - jnp.concatenate([lift, lift], axis=1)
        m = jnp.max(t, axis=0, keepdims=True)
        p = jnp.exp2(t - m)
        total = jnp.sum(p, axis=0, keepdims=True)
        p = p.astype(BF16)
        p_all[blk, :, 2 * k * UD : 2 * (k + 1) * UD] = p
        part = dot(it_t[blk], p)
        for i in range(2):
            s, lanes = ORDER[2 * k + i], slice(i * UD, (i + 1) * UD)
            mst[blk, s : s + 1, :] = m[:, lanes]
            lst[blk, s : s + 1, :] = total[:, lanes]
            acc[blk, s] = part[:, lanes]

    def wait_users(k):
        pltpu.make_async_copy(rows.at[0], rows.at[k], z_rs.at[k]).wait()

    lax.fori_loop(0, 4, arrived, 0)
    c_copy(0).start()
    prepare(0)
    for k in range(1, 4):
        wait_users(k)
    unit(0, 0)
    unit(0, 1)
    lax.fori_loop(4, 8, arrived, 0)
    c_copy(1).start()
    prepare(1)
    qc_copy().wait_recv()
    c_copy(0).wait_recv()
    prepare(2)
    for blk in (1, 2):
        unit(blk, 0)
        unit(blk, 1)
    c_copy(1).wait_recv()
    prepare(3)
    unit(3, 0)
    unit(3, 1)
    for k in (2, 3):
        wait_users(2 * k)
        wait_users(2 * k + 1)
        for blk in range(4):
            unit(blk, k)

    top = jnp.max(mst[...], axis=0)
    local = top + jnp.log2(sum(lst[k] * jnp.exp2(mst[k] - top) for k in range(4)))
    st_out[0] = local

    def st_copy(d):
        return copy(st_out, st_in.at[(NZ - d) % NZ], st_ss.at[d], st_rs.at[(NZ - d) % NZ], dz=d)

    def pt_copy(d):
        return copy(
            pt_out.at[d], pt_in.at[(NZ - d) % NZ], pt_ss.at[d], pt_rs.at[(NZ - d) % NZ], dz=d
        )

    for d in (4, 3, 5, 2, 6, 1, 7):
        st_copy(d).start()

    for k in range(4):
        lst[k] = jnp.exp2(mst[k] - local)

    def part_of(s):
        return sum(acc[k, s] * lst[k, pl.ds(s, 1), :] for k in range(4))

    def give(s, carry):
        pt_out[s] = part_of(s).astype(BF16)
        pt_copy(s).start()
        return carry

    lax.fori_loop(1, NZ, give, 0)

    for e in range(1, NZ):
        pltpu.make_async_copy(st_out, st_in.at[e], st_rs.at[e]).wait()
    seen = [local] + [jnp.roll(st_in[e, 0], e, axis=0) for e in range(1, NZ)]
    top = functools.reduce(jnp.maximum, seen)
    lse = top + jnp.log2(sum(jnp.exp2(v - top) for v in seen))
    share = [jnp.exp2(v[0:1] - lse[0:1]) for v in seen]
    for k in range(4):
        w = jnp.exp2(mst[k] - lse).astype(BF16)
        for i, s in enumerate(ORDER):
            w_row[k, :, i * UD : (i + 1) * UD] = w[s : s + 1, :]

    users_all = rows[...].reshape(NZ * UD, D)

    def item_part(blk):
        return dot(p_all[blk] * w_row[blk], users_all)

    def xc_copy(h):
        part = pl.ds(h * HALF, HALF)
        return copy(ip.at[1, part], xc_in.at[part], xc_ss.at[h], xc_rs.at[h], dc=1)

    for h in (1, 0):
        ip[1, h * HALF : (h + 1) * HALF, :] = item_part(2 + h).astype(BF16)
        xc_copy(h).start()
    for h in (1, 0):
        own_f[h * HALF : (h + 1) * HALF, :] = item_part(h)

    def ls_copy(i, j, **to):
        return copy(loss_out.at[i], loss_in.at[j], ls_ss.at[j], ls_rs.at[j], **to)

    pos_all = st_out[1] + sum(st_in[e, 1] for e in range(1, NZ))
    line = jnp.sum(jnp.sum(lse, axis=1, keepdims=True), axis=0, keepdims=True) * LN2
    loss_out[0] = jnp.broadcast_to(line, (8, 128)) - pos_all
    ls_copy(0, 0, dc=1).start()

    def xs_copy(s, e):
        return copy(
            ip.at[0, pl.ds((s * NX + e) * ID, ID)], xs_in.at[s, NX - e],
            xs_ss.at[s, e], xs_rs.at[s, NX - e], dx=e,
        )

    for h in (1, 0):
        xc_copy(h).wait_recv()

        def own_sum(s, carry):
            spot = pl.ds(pl.multiple_of(s * NX * ID, NX * ID), NX * ID)
            total = own_f[spot, :] + xc_in[spot, :].astype(F32)
            own_f[spot, :] = total
            ip[0, spot, :] = total.astype(BF16)
            for e in (2, 1, 3):
                xs_copy(s, e).start()
            return carry

        lax.fori_loop(h * 4, h * 4 + 4, own_sum, 0)

    ls_copy(0, 0, dc=1).wait_recv()
    loss_out[1] = loss_out[0] + loss_in[0]
    for e in range(1, NX):
        ls_copy(1, e, dx=e).start()

    def ys_copy(s):
        o = offset_of(s)
        mirror = jnp.where(s == 0, 0, jnp.where(s == 7, 7, jnp.where(s % 2 == 1, s + 1, s - 1)))
        return copy(ys_out.at[s], ys_in.at[mirror], ys_ss.at[s], ys_rs.at[mirror], dy=o)

    def x_total(s):
        for e in range(1, NX):
            pltpu.make_async_copy(xs_in.at[s, e], xs_in.at[s, e], xs_rs.at[s, e]).wait()
        spot = pl.ds(pl.multiple_of(s * NX * ID, NX * ID), ID)
        return own_f[spot, :] + sum(xs_in[s, e].astype(F32) for e in range(1, NX))

    def relay(i, carry):
        s = 7 - i
        ys_out[s] = x_total(s).astype(BF16)
        ys_copy(s).start()
        return carry

    lax.fori_loop(0, 7, relay, 0)
    for e in range(1, NX):
        ls_copy(1, e, dx=e).wait_recv()
    loss_out[2] = loss_out[1] + loss_in[1] + loss_in[2] + loss_in[3]
    for d in range(1, NY):
        ls_copy(2, 3 + d, dy=d).start()
    cand = x_total(0) - tq_s[...]

    user_sum = part_of(0) * share[0] - tv_s[...]
    for e in range(1, NZ):
        pltpu.make_async_copy(pt_in.at[e], pt_in.at[e], pt_rs.at[e]).wait()
        user_sum = user_sum + pt_in[e].astype(F32) * share[e]
    query_ref[...] = user_sum.T * (1.0 / scaling_divisor)

    for s in range(1, NY):
        pltpu.make_async_copy(ys_in.at[s], ys_in.at[s], ys_rs.at[s]).wait()
        cand = cand + ys_in[s].astype(F32)
    cand_ref[...] = cand * (1.0 / scaling_divisor)
    total = loss_out[2]
    for d in range(1, NY):
        ls_copy(2, 3 + d, dy=d).wait_recv()
        total = total + loss_in[3 + d]
    loss_ref[...] = total[0:1, 0:1] * (1.0 / (2 * NX * NY * NZ * UD))

    for d in range(1, NZ):
        z_copy(d).wait_send()
        y_copy(d).wait_send()
        ql_copy(d).wait_send()
        st_copy(d).wait_send()
        pt_copy(d).wait_send()
        ls_copy(2, 3 + d, dy=d).wait_send()
    for e in range(1, NX):
        qx_copy(e).wait_send()
        ls_copy(1, e, dx=e).wait_send()

    def left(s, carry):
        for e in range(1, NX):
            x_copy(s, e).wait_send()
            xs_copy(s, e).wait_send()
        return carry

    lax.fori_loop(0, NY, left, 0)

    def left_y(s, carry):
        ys_copy(s).wait_send()
        return carry

    lax.fori_loop(1, NY, left_y, 0)
    for h in range(2):
        c_copy(h).wait_send()
        xc_copy(h).wait_send()
    qc_copy().wait_send()
    ls_copy(0, 0, dc=1).wait_send()


def on_device(users, items, counts, target_indices):
    dma = lambda *n: pltpu.SemaphoreType.DMA(n)
    pair = lambda *n: [dma(*n), dma(*n)]
    vmem = pl.BlockSpec(memory_space=pltpu.VMEM)
    loss, query, cand = pl.pallas_call(
        kernel,
        out_shape=(
            jax.ShapeDtypeStruct((1, 1), F32),
            jax.ShapeDtypeStruct((UD, D), F32),
            jax.ShapeDtypeStruct((ID, D), F32),
        ),
        in_specs=[pl.BlockSpec(memory_space=pl.ANY)] * 4,
        out_specs=(vmem,) * 3,
        scratch_shapes=[
            pltpu.VMEM((UD, D), F32),
            pltpu.VMEM((ID, D), F32),
            pltpu.VMEM((1, ID), jnp.int32),
            pltpu.VMEM((1, UD), jnp.int32),
            dma(4),
            pltpu.VMEM((NZ, UD, D), BF16),
            pltpu.VMEM((2, 2 * HALF, D), BF16),
            pltpu.VMEM((2, NY, NX, 1, 128), F32),
            pltpu.VMEM((4, D, HALF), BF16),
            pltpu.VMEM((4, HALF, 128), F32),
            pltpu.VMEM((4, HALF, NZ * UD), BF16),
            pltpu.VMEM((4, NZ, D, UD), F32),
            pltpu.VMEM((4, NZ, UD), F32),
            pltpu.VMEM((4, NZ, UD), F32),
            pltpu.VMEM((2, 8, 128), F32),
            pltpu.VMEM((NZ, 2, 8, 128), F32),
            pltpu.VMEM((NZ, D, UD), BF16),
            pltpu.VMEM((NZ, D, UD), BF16),
            pltpu.VMEM((4, 1, NZ * UD), BF16),
            pltpu.VMEM((2 * HALF, D), F32),
            pltpu.VMEM((2, 2 * HALF, D), BF16),
            pltpu.VMEM((2 * HALF, D), BF16),
            pltpu.VMEM((NY, NX, ID, D), BF16),
            pltpu.VMEM((NY, ID, D), BF16),
            pltpu.VMEM((NY, ID, D), BF16),
            pltpu.VMEM((3, 8, 128), F32),
            pltpu.VMEM((11, 8, 128), F32),
            pltpu.VMEM((ID, D), F32),
            pltpu.VMEM((D, UD), F32),
            *pair(NZ), *pair(NY), *pair(NY), *pair(NY, NX), *pair(NX), *pair(3),
            *pair(NZ), *pair(NZ), *pair(2), *pair(NY, NX), *pair(NY), *pair(11),
        ],
        compiler_params=pltpu.CompilerParams(
            collective_id=0, has_side_effects=True, vmem_limit_bytes=48 * 2**20
        ),
        cost_estimate=pl.CostEstimate(
            flops=6 * 1024 * 2048 * D, bytes_accessed=2**19, transcendentals=1024 * 2048
        ),
        name="towers",
    )(users, items, counts.reshape(1, ID), target_indices.reshape(1, UD))
    return loss.reshape(()), query, cand


def solution(mesh):
    placed = P(("blk", "grp"))
    wide = P(("blk", "grp"), None)
    return jax.shard_map(
        on_device,
        mesh=mesh,
        in_specs=(wide, wide, placed, placed),
        out_specs=(P(), wide, wide),
        check_vma=False,
    )
```

```python
import functools
import math

import jax
import jax.numpy as jnp
from jax import lax
from jax.experimental import pallas as pl
from jax.experimental.pallas import tpu as pltpu
from jax.sharding import PartitionSpec as P

scaling_divisor = 5.0
LOG2E = math.log2(math.e)
LN2 = math.log(2.0)
MESH = pl.DeviceIdType.MESH
BF16 = jnp.bfloat16
F32 = jnp.float32

NX, NY, NZ = 4, 8, 8
UD, ID, D = 128, 32, 256
ORDER = (0, 1, 7, 2, 6, 3, 5, 4)
SLOT = tuple(ORDER.index(k) for k in range(NY))
HALF = NX * NY * ID // 2


def dot(a, b, ca=1, cb=0):
    return lax.dot_general(a, b, (((ca,), (cb,)), ((), ())), preferred_element_type=F32)


def kernel(
    users_hbm, items_hbm, counts_hbm, tgt_hbm,
    loss_ref, query_ref, cand_ref,
    users_ref, items_ref, counts_ref, tgt_ref, in_sem,
    rows, it, lq, it_t, lqc, p_all, acc, mst, lst, st_out, st_in, pt_out, pt_in,
    w_row, own_f, ip, xc_in, xs_in, ys_out, ys_in, loss_out, loss_in, tq_s, tv_s,
    sent, z_rs, y_rs, x_rs, c_rs, xc_rs, xs_rs, got,
):
    b = lax.axis_index("blk")
    g = lax.axis_index("grp")
    x = (b // 16) * 2 + g % 2
    y = (b // 2) % 8
    z = g // 2
    core = b % 2

    def device(dx=0, dy=0, dz=0, dc=0):
        xx = (x + dx) % NX
        return (
            ((xx // 2) * 8 + (y + dy) % NY) * 2 + (core + dc) % 2,
            ((z + dz) % NZ) * 2 + xx % 2,
        )

    Z_S, Y_S, QL_S, X_S, QX_S, C_S, QC_S, ST_S, PT_S, XC_S, XS_S, YS_S, L0_S, L1_S, L2_S = (
        sent.at[k] for k in range(15)
    )
    QL_R, QX_R, QC_R, ST_R, PT_R, YS_R, L0_R, L1_R, L2_R = (got.at[k] for k in range(9))

    def whole(ref, sem):
        pltpu.make_async_copy(ref, ref, sem).wait()

    def copy(src, dst, ss, rs, **to):
        return pltpu.make_async_remote_copy(
            src_ref=src, dst_ref=dst, send_sem=ss, recv_sem=rs,
            device_id=device(**to), device_id_type=MESH,
        )

    barrier = pltpu.get_barrier_semaphore()
    for d in range(1, NZ):
        pl.semaphore_signal(barrier, inc=1, device_id=device(dz=d), device_id_type=MESH)
    for d in range(1, NY):
        pl.semaphore_signal(barrier, inc=1, device_id=device(dy=d), device_id_type=MESH)
    for d in range(1, NX):
        pl.semaphore_signal(barrier, inc=1, device_id=device(dx=d), device_id_type=MESH)
    pl.semaphore_signal(barrier, inc=1, device_id=device(dc=1), device_id_type=MESH)

    loads = [
        pltpu.make_async_copy(src, dst, in_sem.at[k])
        for k, (src, dst) in enumerate((
            (counts_hbm, counts_ref), (items_hbm, items_ref), (users_hbm, users_ref), (tgt_hbm, tgt_ref)
        ))
    ]
    for load in loads:
        load.start()
    for load in loads:
        load.wait()
    rows[0] = users_ref[...].astype(BF16)
    it[0, 0:ID, :] = items_ref[...].astype(BF16)
    logq = jnp.log(counts_ref[...].astype(F32)).astype(BF16).astype(F32)
    logq = jnp.concatenate([logq, jnp.zeros((1, 128 - ID), F32)], axis=1)
    lq[0, 0, 0] = logq

    pl.semaphore_wait(barrier, NZ + NY + NX - 3 + 1)

    def z_copy(d):
        s = SLOT[(NZ - d) % NZ]
        return copy(rows.at[0], rows.at[s], Z_S, z_rs.at[s // 2], dz=d)

    def y_copy(d):
        s = SLOT[(NY - d) % NY]
        return copy(
            it.at[0, pl.ds(0, ID)], it.at[0, pl.ds(s * NX * ID, ID)], Y_S, y_rs.at[s], dy=d
        )

    def ql_copy(d):
        s = SLOT[(NY - d) % NY]
        return copy(lq.at[0, 0, 0], lq.at[0, s, 0], QL_S, QL_R, dy=d)

    def x_copy(s, e):
        return copy(
            it.at[0, pl.ds(s * NX * ID, ID)],
            it.at[0, pl.ds((s * NX + NX - e) * ID, ID)],
            X_S, x_rs.at[s], dx=e,
        )

    def qx_copy(e):
        return copy(lq.at[0, :, 0], lq.at[0, :, NX - e], QX_S, QX_R, dx=e)

    def c_copy(s):
        part = pl.ds(s * NX * ID, NX * ID)
        return copy(it.at[0, part], it.at[1, part], C_S, c_rs.at[s // 4], dc=1)

    def qc_copy():
        return copy(lq.at[0], lq.at[1], QC_S, QC_R, dc=1)

    for d in ORDER[1:]:
        ql_copy(d).start()
    for d in ORDER[1:]:
        y_copy(d).start()
    for e in range(1, NX):
        x_copy(0, e).start()
    for d in ORDER[1:]:
        z_copy(d).start()

    def forward(s):
        whole(it.at[0, pl.ds(s * NX * ID, ID)], y_rs.at[s])
        for e in range(1, NX):
            x_copy(s, e).start()

    for s in range(1, 4):
        forward(s)
    whole(lq.at[0, 1:NY, 0], QL_R)
    for e in range(1, NX):
        qx_copy(e).start()
    for s in range(4, 8):
        forward(s)

    first = (b * 16 + g) * ID
    hot = (
        lax.broadcasted_iota(jnp.int32, (ID, UD), 0) + first == tgt_ref[...]
    ).astype(F32)
    hot_half = hot.astype(BF16)
    own_items = it[0, 0:ID, :]
    tq = dot(hot_half, rows[0])
    tq_s[...] = tq
    tv_s[...] = dot(own_items, hot_half, 0, 0)
    eye = (
        lax.broadcasted_iota(jnp.int32, (ID, 128), 0)
        == lax.broadcasted_iota(jnp.int32, (ID, 128), 1)
    )
    own_logq = jnp.where(eye, jnp.broadcast_to(logq, (ID, 128)), 0.0)
    named = jnp.sum(hot, axis=1, keepdims=True)
    pos = jnp.sum(
        jnp.sum(tq * own_items.astype(F32), axis=1, keepdims=True) * (1.0 / scaling_divisor)
        - jnp.sum(own_logq, axis=1, keepdims=True) * named,
        axis=0, keepdims=True,
    )
    st_out[1] = jnp.broadcast_to(pos, (8, 128))

    def arrived(s):
        whole(it.at[0, pl.ds((s * NX + 1) * ID, 3 * ID)], x_rs.at[s])
        c_copy(s).start()

    ones = jnp.ones((128, 128), BF16)

    def prepare(blk):
        side, half = blk // 2, blk % 2
        it_t[blk] = it[side, half * HALF : (half + 1) * HALF, :].T
        row = lq[side, half * 4 : (half + 1) * 4].reshape(16, 1, 128)
        spread = jnp.where(eye[None], jnp.broadcast_to(row, (16, ID, 128)), 0.0)
        lqc[blk] = dot(spread.reshape(HALF, 128).astype(BF16), ones) * LOG2E

    def unit(blk, k):
        side, half = blk // 2, blk % 2
        pair = rows[2 * k : 2 * k + 2].reshape(2 * UD, D)
        scores = dot(it[side, half * HALF : (half + 1) * HALF, :], pair, 1, 1)
        lift = lqc[blk]
        t = scores * (LOG2E / scaling_divisor) - jnp.concatenate([lift, lift], axis=1)
        m = jnp.max(t, axis=0, keepdims=True)
        p = jnp.exp2(t - m)
        total = jnp.sum(p, axis=0, keepdims=True)
        p = p.astype(BF16)
        p_all[blk, :, 2 * k * UD : 2 * (k + 1) * UD] = p
        part = dot(it_t[blk], p)
        for i in range(2):
            s, lanes = ORDER[2 * k + i], slice(i * UD, (i + 1) * UD)
            mst[blk, s : s + 1, :] = m[:, lanes]
            lst[blk, s : s + 1, :] = total[:, lanes]
            acc[blk, s] = part[:, lanes]

    def wait_users(k):
        whole(rows.at[max(2 * k, 1) : 2 * k + 2], z_rs.at[k])

    for s in range(4):
        arrived(s)
    whole(lq.at[0, :, 1:NX], QX_R)
    qc_copy().start()
    prepare(0)
    wait_users(0)
    wait_users(1)
    unit(0, 0)
    unit(0, 1)
    for s in range(4, 8):
        arrived(s)
    qc_copy().wait_recv()
    whole(it.at[1, pl.ds(0, HALF)], c_rs.at[0])
    prepare(1)
    prepare(2)
    for blk in (1, 2):
        unit(blk, 0)
        unit(blk, 1)
    whole(it.at[1, pl.ds(HALF, HALF)], c_rs.at[1])
    prepare(3)
    unit(3, 0)
    unit(3, 1)
    for k in (2, 3):
        wait_users(k)
        for blk in range(4):
            unit(blk, k)

    top = jnp.max(mst[...], axis=0)
    local = top + jnp.log2(sum(lst[k] * jnp.exp2(mst[k] - top) for k in range(4)))
    st_out[0] = local

    def st_copy(d):
        return copy(st_out, st_in.at[(NZ - d) % NZ], ST_S, ST_R, dz=d)

    def pt_copy(d):
        return copy(pt_out.at[d], pt_in.at[(NZ - d) % NZ], PT_S, PT_R, dz=d)

    for d in (4, 3, 5, 2, 6, 1, 7):
        st_copy(d).start()

    for k in range(4):
        lst[k] = jnp.exp2(mst[k] - local)

    def part_of(s):
        return sum(acc[k, s] * lst[k, pl.ds(s, 1), :] for k in range(4))

    def give(s, carry):
        pt_out[s] = part_of(s).astype(BF16)
        pt_copy(s).start()
        return carry

    lax.fori_loop(1, NZ, give, 0)

    whole(rows.at[1:NZ], Z_S)
    whole(it.at[0, pl.ds(0, 7 * ID)], Y_S)
    whole(lq.at[0, 1:NY, 0], QL_S)
    whole(it.at[0, pl.ds(0, 24 * ID)], X_S)
    whole(lq.at[0, :, 1:NX], QX_S)
    whole(it.at[0], C_S)
    whole(lq.at[0], QC_S)

    whole(st_in.at[1:NZ], ST_R)
    seen = [local] + [jnp.roll(st_in[e, 0], e, axis=0) for e in range(1, NZ)]
    top = functools.reduce(jnp.maximum, seen)
    lse = top + jnp.log2(sum(jnp.exp2(v - top) for v in seen))
    share = [jnp.exp2(v[0:1] - lse[0:1]) for v in seen]
    for k in range(4):
        w = jnp.exp2(mst[k] - lse).astype(BF16)
        for i, s in enumerate(ORDER):
            w_row[k, :, i * UD : (i + 1) * UD] = w[s : s + 1, :]

    users_all = rows[...].reshape(NZ * UD, D)

    def item_part(blk):
        return dot(p_all[blk] * w_row[blk], users_all)

    def xc_copy(h):
        part = pl.ds(h * HALF, HALF)
        return copy(ip.at[1, part], xc_in.at[part], XC_S, xc_rs.at[h], dc=1)

    for h in (1, 0):
        ip[1, h * HALF : (h + 1) * HALF, :] = item_part(2 + h).astype(BF16)
        xc_copy(h).start()
    for h in (1, 0):
        own_f[h * HALF : (h + 1) * HALF, :] = item_part(h)

    def ls_copy(i, j, **to):
        ss, rs = ((L0_S, L0_R), (L1_S, L1_R), (L2_S, L2_R))[i]
        return copy(loss_out.at[i], loss_in.at[j], ss, rs, **to)

    pos_all = st_out[1] + sum(st_in[e, 1] for e in range(1, NZ))
    line = jnp.sum(jnp.sum(lse, axis=1, keepdims=True), axis=0, keepdims=True) * LN2
    loss_out[0] = jnp.broadcast_to(line, (8, 128)) - pos_all
    ls_copy(0, 0, dc=1).start()

    def xs_copy(s, e):
        return copy(
            ip.at[0, pl.ds((s * NX + e) * ID, ID)], xs_in.at[s, NX - e],
            XS_S, xs_rs.at[s], dx=e,
        )

    for h in (1, 0):
        xc_copy(h).wait_recv()
        for k in range(h * 4 + 3, h * 4 - 1, -1):
            spot = slice(k * NX * ID, (k + 1) * NX * ID)
            total = own_f[spot, :] + xc_in[spot, :].astype(F32)
            own_f[spot, :] = total
            ip[0, spot, :] = total.astype(BF16)
            for e in (2, 1, 3):
                xs_copy(k, e).start()

    whole(loss_in.at[0], L0_R)
    loss_out[1] = loss_out[0] + loss_in[0]
    for e in range(1, NX):
        ls_copy(1, e, dx=e).start()

    def ys_copy(s):
        mirror = SLOT[(NY - ORDER[s]) % NY]
        return copy(
            ys_out.at[s], ys_in.at[mirror], YS_S, YS_R, dy=ORDER[s]
        )

    def x_total(s):
        whole(xs_in.at[s, 1:NX], xs_rs.at[s])
        spot = slice(s * NX * ID, s * NX * ID + ID)
        return own_f[spot, :] + sum(xs_in[s, e].astype(F32) for e in range(1, NX))

    for s in range(NY - 1, 0, -1):
        ys_out[s] = x_total(s).astype(BF16)
        ys_copy(s).start()
    whole(loss_in.at[1:NX], L1_R)
    loss_out[2] = loss_out[1] + loss_in[1] + loss_in[2] + loss_in[3]
    for d in range(1, NY):
        ls_copy(2, 3 + d, dy=d).start()
    cand = x_total(0) - tq_s[...]

    user_sum = part_of(0) * share[0] - tv_s[...]
    whole(pt_in.at[1:NZ], PT_R)
    for e in range(1, NZ):
        user_sum = user_sum + pt_in[e].astype(F32) * share[e]
    query_ref[...] = user_sum.T * (1.0 / scaling_divisor)
    whole(st_in.at[1:NZ], ST_S)
    whole(pt_in.at[1:NZ], PT_S)
    whole(ip.at[1], XC_S)
    whole(xs_in.at[:, 1:NX], XS_S)
    whole(loss_in.at[0], L0_S)
    whole(loss_in.at[1:NX], L1_S)

    whole(ys_in.at[1:NY], YS_R)
    for s in range(1, NY):
        cand = cand + ys_in[s].astype(F32)
    cand_ref[...] = cand * (1.0 / scaling_divisor)
    total = loss_out[2]
    whole(loss_in.at[4:11], L2_R)
    for d in range(1, NY):
        total = total + loss_in[3 + d]
    loss_ref[...] = total[0:1, 0:1] * (1.0 / (2 * NX * NY * NZ * UD))

    whole(ys_in.at[1:NY], YS_S)
    whole(loss_in.at[4:11], L2_S)


def on_device(users, items, counts, target_indices):
    dma = lambda *n: pltpu.SemaphoreType.DMA(n)
    vmem = pl.BlockSpec(memory_space=pltpu.VMEM)
    loss, query, cand = pl.pallas_call(
        kernel,
        out_shape=(
            jax.ShapeDtypeStruct((1, 1), F32),
            jax.ShapeDtypeStruct((UD, D), F32),
            jax.ShapeDtypeStruct((ID, D), F32),
        ),
        in_specs=[pl.BlockSpec(memory_space=pltpu.HBM)] * 4,
        out_specs=(vmem,) * 3,
        scratch_shapes=[
            pltpu.VMEM((UD, D), F32),
            pltpu.VMEM((ID, D), F32),
            pltpu.VMEM((1, ID), jnp.int32),
            pltpu.VMEM((1, UD), jnp.int32),
            dma(4),
            pltpu.VMEM((NZ, UD, D), BF16),
            pltpu.VMEM((2, 2 * HALF, D), BF16),
            pltpu.VMEM((2, NY, NX, 1, 128), F32),
            pltpu.VMEM((4, D, HALF), BF16),
            pltpu.VMEM((4, HALF, 128), F32),
            pltpu.VMEM((4, HALF, NZ * UD), BF16),
            pltpu.VMEM((4, NZ, D, UD), F32),
            pltpu.VMEM((4, NZ, UD), F32),
            pltpu.VMEM((4, NZ, UD), F32),
            pltpu.VMEM((2, 8, 128), F32),
            pltpu.VMEM((NZ, 2, 8, 128), F32),
            pltpu.VMEM((NZ, D, UD), BF16),
            pltpu.VMEM((NZ, D, UD), BF16),
            pltpu.VMEM((4, 1, NZ * UD), BF16),
            pltpu.VMEM((2 * HALF, D), F32),
            pltpu.VMEM((2, 2 * HALF, D), BF16),
            pltpu.VMEM((2 * HALF, D), BF16),
            pltpu.VMEM((NY, NX, ID, D), BF16),
            pltpu.VMEM((NY, ID, D), BF16),
            pltpu.VMEM((NY, ID, D), BF16),
            pltpu.VMEM((3, 8, 128), F32),
            pltpu.VMEM((11, 8, 128), F32),
            pltpu.VMEM((ID, D), F32),
            pltpu.VMEM((D, UD), F32),
            dma(15), dma(NZ // 2), dma(NY), dma(NY), dma(2), dma(2), dma(NY), dma(9),
        ],
        compiler_params=pltpu.CompilerParams(
            collective_id=0, has_side_effects=True, vmem_limit_bytes=64 * 2**20
        ),
        cost_estimate=pl.CostEstimate(
            flops=6 * 1024 * 2048 * D, bytes_accessed=2**19, transcendentals=1024 * 2048
        ),
        name="towers",
    )(users, items, counts.reshape(1, ID), target_indices.reshape(1, UD))
    return loss.reshape(()), query, cand


def solution(mesh):
    placed = P(("blk", "grp"))
    wide = P(("blk", "grp"), None)
    return jax.shard_map(
        on_device,
        mesh=mesh,
        in_specs=(wide, wide, placed, placed),
        out_specs=(P(), wide, wide),
        check_vma=False,
    )
```

```python
import functools
import math

import jax
import jax.numpy as jnp
from jax import lax
from jax.experimental import pallas as pl
from jax.experimental.pallas import tpu as pltpu
from jax.sharding import PartitionSpec as P

scaling_divisor = 5.0
LOG2E = math.log2(math.e)
LN2 = math.log(2.0)
MESH = pl.DeviceIdType.MESH
BF16 = jnp.bfloat16
F32 = jnp.float32

NX, NY, NZ = 4, 8, 8
UD, ID, D = 128, 32, 256
ORDER = (0, 1, 7, 2, 6, 3, 5, 4)
SLOT = tuple(ORDER.index(k) for k in range(NY))
HALF = NX * NY * ID // 2
BLOCKS = tuple((i, r, n) for i in range(2) for r, n in ((0, 512), (512, 256), (768, 256)))
NB = len(BLOCKS)


def dot(a, b, ca=1, cb=0):
    return lax.dot_general(a, b, (((ca,), (cb,)), ((), ())), preferred_element_type=F32)


def kernel(
    users_hbm, items_hbm, counts_hbm, tgt_hbm,
    loss_ref, query_hbm, cand_hbm,
    query_ref, cand_ref,
    users_ref, items_ref, counts_ref, tgt_ref, in_sem,
    rows, it, lq, it_t, lqc, p_all, acc, mst, lst, st_out, st_in, pt_out, pt_in,
    w_row, own_f, ip, xc_in, xs_in, ys_out, ys_in, loss_out, loss_in, tq_s, tv_s,
    sent, z_rs, y_rs, x_rs, c_rs, xc_rs, xs_rs, got, out_sem,
):
    b = lax.axis_index("blk")
    g = lax.axis_index("grp")
    x = (b // 16) * 2 + g % 2
    y = (b // 2) % 8
    z = g // 2
    core = b % 2

    def device(dx=0, dy=0, dz=0, dc=0):
        xx = (x + dx) % NX
        return (
            ((xx // 2) * 8 + (y + dy) % NY) * 2 + (core + dc) % 2,
            ((z + dz) % NZ) * 2 + xx % 2,
        )

    Z_S, Y_S, QL_S, X_S, QX_S, C_S, QC_S, ST_S, PT_S, XC_S, XS_S, YS_S, L0_S, L1_S, L2_S = (
        sent.at[k] for k in range(15)
    )
    QL_R, QX_R, QC_R, ST_R, PT_R, YS_R, L0_R, L1_R, L2_R = (got.at[k] for k in range(9))

    def whole(ref, sem):
        pltpu.make_async_copy(ref, ref, sem).wait()

    def copy(src, dst, ss, rs, **to):
        return pltpu.make_async_remote_copy(
            src_ref=src, dst_ref=dst, send_sem=ss, recv_sem=rs,
            device_id=device(**to), device_id_type=MESH,
        )

    loads = [
        pltpu.make_async_copy(src, dst, in_sem.at[k])
        for k, (src, dst) in enumerate((
            (counts_hbm, counts_ref), (items_hbm, items_ref), (users_hbm, users_ref), (tgt_hbm, tgt_ref)
        ))
    ]
    for load in loads:
        load.start()

    barrier = pltpu.get_barrier_semaphore()
    for d in range(1, NZ):
        pl.semaphore_signal(barrier, inc=1, device_id=device(dz=d), device_id_type=MESH)
    for d in range(1, NY):
        pl.semaphore_signal(barrier, inc=1, device_id=device(dy=d), device_id_type=MESH)
    for d in range(1, NX):
        pl.semaphore_signal(barrier, inc=1, device_id=device(dx=d), device_id_type=MESH)
    pl.semaphore_signal(barrier, inc=1, device_id=device(dc=1), device_id_type=MESH)

    loads[0].wait()
    loads[1].wait()
    it[0, 0:ID, :] = items_ref[...].astype(BF16)
    logq = jnp.log(counts_ref[...].astype(F32)).astype(BF16).astype(F32)
    logq = jnp.concatenate([logq, jnp.zeros((1, 128 - ID), F32)], axis=1)
    lq[0, 0, 0] = logq

    pl.semaphore_wait(barrier, NZ + NY + NX - 3 + 1)

    def z_copy(d):
        s = SLOT[(NZ - d) % NZ]
        return copy(rows.at[0], rows.at[s], Z_S, z_rs.at[s // 2], dz=d)

    def y_copy(d):
        s = SLOT[(NY - d) % NY]
        return copy(
            it.at[0, pl.ds(0, ID)], it.at[0, pl.ds(s * NX * ID, ID)], Y_S, y_rs.at[s], dy=d
        )

    def ql_copy(d):
        s = SLOT[(NY - d) % NY]
        return copy(lq.at[0, 0, 0], lq.at[0, s, 0], QL_S, QL_R, dy=d)

    def x_copy(s, e):
        return copy(
            it.at[0, pl.ds(s * NX * ID, ID)],
            it.at[0, pl.ds((s * NX + NX - e) * ID, ID)],
            X_S, x_rs.at[s], dx=e,
        )

    def qx_copy(e):
        return copy(lq.at[0, :, 0], lq.at[0, :, NX - e], QX_S, QX_R, dx=e)

    def c_copy(s):
        part = pl.ds(s * NX * ID, NX * ID)
        return copy(it.at[0, part], it.at[1, part], C_S, c_rs.at[max(s // 2 - 1, 0)], dc=1)

    def qc_copy():
        return copy(lq.at[0], lq.at[1], QC_S, QC_R, dc=1)

    for d in (4, 1, 7, 3, 5, 2, 6):
        y_copy(d).start()
    for d in (4, 1, 7, 3, 5, 2, 6):
        ql_copy(d).start()
    for e in range(1, NX):
        x_copy(0, e).start()
    loads[2].wait()
    rows[0] = users_ref[...].astype(BF16)
    for d in ORDER[1:]:
        z_copy(d).start()

    def forward(s):
        whole(it.at[0, pl.ds(s * NX * ID, ID)], y_rs.at[s])
        for e in range(1, NX):
            x_copy(s, e).start()

    for s in range(1, 4):
        forward(s)
    whole(lq.at[0, 1:NY, 0], QL_R)
    for e in range(1, NX):
        qx_copy(e).start()
    for s in range(4, 8):
        forward(s)

    first = (b * 16 + g) * ID
    loads[3].wait()
    hot = (
        lax.broadcasted_iota(jnp.int32, (ID, UD), 0) + first == tgt_ref[...]
    ).astype(F32)
    hot_half = hot.astype(BF16)
    own_items = it[0, 0:ID, :]
    tq = dot(hot_half, rows[0])
    tq_s[...] = tq
    tv_s[...] = dot(own_items, hot_half, 0, 0)
    eye = (
        lax.broadcasted_iota(jnp.int32, (ID, 128), 0)
        == lax.broadcasted_iota(jnp.int32, (ID, 128), 1)
    )
    own_logq = jnp.where(eye, jnp.broadcast_to(logq, (ID, 128)), 0.0)
    named = jnp.sum(hot, axis=1, keepdims=True)
    pos = jnp.sum(
        jnp.sum(tq * own_items.astype(F32), axis=1, keepdims=True) * (1.0 / scaling_divisor)
        - jnp.sum(own_logq, axis=1, keepdims=True) * named,
        axis=0, keepdims=True,
    )
    st_out[1] = jnp.broadcast_to(pos, (8, 128))

    def arrived(s):
        whole(it.at[0, pl.ds((s * NX + 1) * ID, 3 * ID)], x_rs.at[s])
        c_copy(s).start()

    ones = jnp.ones((128, 128), BF16)

    def spot_of(blk):
        side, row, n = BLOCKS[blk]
        return slice(side * 2 * HALF + row, side * 2 * HALF + row + n)

    def prepare(blk):
        side, row, n = BLOCKS[blk]
        it_t[:, spot_of(blk)] = it[side, row : row + n, :].T
        shards = n // ID
        first_slot = row // (NX * ID)
        found = lq[side, first_slot : first_slot + shards // NX].reshape(shards, 1, 128)
        spread = jnp.where(eye[None], jnp.broadcast_to(found, (shards, ID, 128)), 0.0)
        lqc[spot_of(blk), :] = dot(spread.reshape(n, 128).astype(BF16), ones) * LOG2E

    def unit(blk, k):
        side, row, n = BLOCKS[blk]
        pair = rows[2 * k : 2 * k + 2].reshape(2 * UD, D)
        scores = dot(it[side, row : row + n, :], pair, 1, 1)
        lift = lqc[spot_of(blk), :]
        t = scores * (LOG2E / scaling_divisor) - jnp.concatenate([lift, lift], axis=1)
        m = jnp.max(t, axis=0, keepdims=True)
        p = jnp.exp2(t - m)
        total = jnp.sum(p, axis=0, keepdims=True)
        p_all[spot_of(blk), 2 * k * UD : 2 * (k + 1) * UD] = p.astype(BF16)
        for i in range(2):
            s, lanes = ORDER[2 * k + i], slice(i * UD, (i + 1) * UD)
            mst[blk, s : s + 1, :] = m[:, lanes]
            lst[blk, s : s + 1, :] = total[:, lanes]

    def weighted(blk, k):
        part = dot(it_t[:, spot_of(blk)], p_all[spot_of(blk), 2 * k * UD : 2 * (k + 1) * UD])
        for i in range(2):
            acc[blk, ORDER[2 * k + i]] = part[:, i * UD : (i + 1) * UD]

    def wait_users(k):
        whole(rows.at[max(2 * k, 1) : 2 * k + 2], z_rs.at[k])

    def wait_other(k):
        row, n = ((0, 512), (512, 256), (768, 256))[k]
        whole(it.at[1, pl.ds(row, n)], c_rs.at[k])

    for s in range(4):
        arrived(s)
    whole(lq.at[0, :, 1:NX], QX_R)
    qc_copy().start()
    prepare(0)
    wait_users(0)
    wait_users(1)
    unit(0, 0)
    unit(0, 1)
    arrived(4)
    arrived(5)
    qc_copy().wait_recv()
    wait_other(0)
    prepare(1)
    prepare(3)
    for blk in (1, 3):
        unit(blk, 0)
        unit(blk, 1)
    arrived(6)
    arrived(7)
    prepare(2)
    unit(2, 0)
    unit(2, 1)
    for k in (2, 3):
        wait_users(k)
        for blk in range(4):
            unit(blk, k)
    for blk in (4, 5):
        wait_other(blk - 3)
        prepare(blk)
        for k in range(4):
            unit(blk, k)

    top = jnp.max(mst[...], axis=0)
    local = top + jnp.log2(sum(lst[k] * jnp.exp2(mst[k] - top) for k in range(NB)))
    st_out[0] = local

    def st_copy(d):
        return copy(st_out, st_in.at[(NZ - d) % NZ], ST_S, ST_R, dz=d)

    def pt_copy(d):
        return copy(pt_out.at[d], pt_in.at[(NZ - d) % NZ], PT_S, PT_R, dz=d)

    for d in (4, 3, 5, 2, 6, 1, 7):
        st_copy(d).start()

    for k in range(NB):
        lst[k] = jnp.exp2(mst[k] - local)
    for k in (3, 2, 1, 0):
        for blk in range(NB):
            weighted(blk, k)

    def part_of(s):
        return sum(acc[k, s] * lst[k, pl.ds(s, 1), :] for k in range(NB))

    def give(s, carry):
        pt_out[s] = part_of(s).astype(BF16)
        pt_copy(s).start()
        return carry

    lax.fori_loop(1, NZ, give, 0)

    whole(rows.at[1:NZ], Z_S)
    whole(it.at[0, pl.ds(0, 7 * ID)], Y_S)
    whole(lq.at[0, 1:NY, 0], QL_S)
    whole(it.at[0, pl.ds(0, 24 * ID)], X_S)
    whole(lq.at[0, :, 1:NX], QX_S)
    whole(it.at[0], C_S)
    whole(lq.at[0], QC_S)

    whole(st_in.at[1:NZ], ST_R)
    seen = [local] + [jnp.roll(st_in[e, 0], e, axis=0) for e in range(1, NZ)]
    top = functools.reduce(jnp.maximum, seen)
    lse = top + jnp.log2(sum(jnp.exp2(v - top) for v in seen))
    share = [jnp.exp2(v[0:1] - lse[0:1]) for v in seen]
    for k in range(NB):
        w = jnp.exp2(mst[k] - lse).astype(BF16)
        for i, s in enumerate(ORDER):
            w_row[k, :, i * UD : (i + 1) * UD] = w[s : s + 1, :]

    users_all = rows[...].reshape(NZ * UD, D)

    def item_part(blk, row, n):
        return dot(p_all[row : row + n, :] * w_row[blk], users_all)

    QUARTER = HALF // 2

    def xc_copy(c):
        part = pl.ds(c * QUARTER, QUARTER)
        return copy(ip.at[1, part], xc_in.at[part], XC_S, xc_rs.at[c], dc=1)

    for c, blk in ((3, 5), (2, 4), (1, 3), (0, 3)):
        part = item_part(blk, 2 * HALF + c * QUARTER, QUARTER)
        ip[1, c * QUARTER : (c + 1) * QUARTER, :] = part.astype(BF16)
        xc_copy(c).start()
    for blk in (2, 1, 0):
        own_f[spot_of(blk), :] = item_part(blk, BLOCKS[blk][1], BLOCKS[blk][2])

    def ls_copy(i, j, **to):
        ss, rs = ((L0_S, L0_R), (L1_S, L1_R), (L2_S, L2_R))[i]
        return copy(loss_out.at[i], loss_in.at[j], ss, rs, **to)

    pos_all = st_out[1] + sum(st_in[e, 1] for e in range(1, NZ))
    line = jnp.sum(jnp.sum(lse, axis=1, keepdims=True), axis=0, keepdims=True) * LN2
    loss_out[0] = jnp.broadcast_to(line, (8, 128)) - pos_all
    ls_copy(0, 0, dc=1).start()

    def xs_copy(s, e):
        return copy(
            ip.at[0, pl.ds((s * NX + e) * ID, ID)], xs_in.at[s, NX - e],
            XS_S, xs_rs.at[s], dx=e,
        )

    for c in (3, 2, 1, 0):
        xc_copy(c).wait_recv()
        for k in (2 * c + 1, 2 * c):
            spot = slice(k * NX * ID, (k + 1) * NX * ID)
            total = own_f[spot, :] + xc_in[spot, :].astype(F32)
            own_f[spot, :] = total
            ip[0, spot, :] = total.astype(BF16)
            for e in (2, 1, 3):
                xs_copy(k, e).start()

    whole(loss_in.at[0], L0_R)
    loss_out[1] = loss_out[0] + loss_in[0]
    for e in range(1, NX):
        ls_copy(1, e, dx=e).start()

    def ys_copy(s):
        mirror = SLOT[(NY - ORDER[s]) % NY]
        return copy(
            ys_out.at[s], ys_in.at[mirror], YS_S, YS_R, dy=ORDER[s]
        )

    def x_total(s):
        whole(xs_in.at[s, 1:NX], xs_rs.at[s])
        spot = slice(s * NX * ID, s * NX * ID + ID)
        return own_f[spot, :] + sum(xs_in[s, e].astype(F32) for e in range(1, NX))

    for s in range(NY - 1, 0, -1):
        ys_out[s] = x_total(s).astype(BF16)
        ys_copy(s).start()
    whole(loss_in.at[1:NX], L1_R)
    loss_out[2] = loss_out[1] + loss_in[1] + loss_in[2] + loss_in[3]
    for d in range(1, NY):
        ls_copy(2, 3 + d, dy=d).start()
    cand = x_total(0) - tq_s[...]

    user_sum = part_of(0) * share[0] - tv_s[...]
    whole(pt_in.at[1:NZ], PT_R)
    for e in range(1, NZ):
        user_sum = user_sum + pt_in[e].astype(F32) * share[e]
    query_ref[...] = user_sum.T * (1.0 / scaling_divisor)
    query_out = pltpu.make_async_copy(query_ref, query_hbm, out_sem.at[0])
    query_out.start()
    whole(st_in.at[1:NZ], ST_S)
    whole(pt_in.at[1:NZ], PT_S)
    whole(ip.at[1], XC_S)
    whole(xs_in.at[:, 1:NX], XS_S)
    whole(loss_in.at[0], L0_S)
    whole(loss_in.at[1:NX], L1_S)

    whole(ys_in.at[1:NY], YS_R)
    for s in range(1, NY):
        cand = cand + ys_in[s].astype(F32)
    cand_ref[...] = cand * (1.0 / scaling_divisor)
    cand_out = pltpu.make_async_copy(cand_ref, cand_hbm, out_sem.at[1])
    cand_out.start()
    total = loss_out[2]
    whole(loss_in.at[4:11], L2_R)
    for d in range(1, NY):
        total = total + loss_in[3 + d]
    loss_ref[...] = total[0:1, 0:1] * (1.0 / (2 * NX * NY * NZ * UD))

    whole(ys_in.at[1:NY], YS_S)
    whole(loss_in.at[4:11], L2_S)
    query_out.wait()
    cand_out.wait()


def settle(
    loss_in, query_in, cand_in, loss_out, query_out, cand_out, query_v, cand_v, in_sem, out_sem
):
    ins = [
        pltpu.make_async_copy(query_in, query_v, in_sem.at[0]),
        pltpu.make_async_copy(cand_in, cand_v, in_sem.at[1]),
    ]
    outs = [
        pltpu.make_async_copy(query_v, query_out, out_sem.at[0]),
        pltpu.make_async_copy(cand_v, cand_out, out_sem.at[1]),
    ]
    for move in ins:
        move.start()
    loss_out[...] = loss_in[...]
    for arrival, departure in zip(ins, outs):
        arrival.wait()
        departure.start()
    for departure in outs:
        departure.wait()


def on_device(users, items, counts, target_indices):
    dma = lambda *n: pltpu.SemaphoreType.DMA(n)
    anywhere = pl.BlockSpec(memory_space=pl.ANY)
    results = (
        jax.ShapeDtypeStruct((1, 1), F32),
        jax.ShapeDtypeStruct((UD, D), F32),
        jax.ShapeDtypeStruct((ID, D), F32),
    )
    found = pl.pallas_call(
        kernel,
        out_shape=results,
        in_specs=[anywhere] * 4,
        out_specs=(pl.BlockSpec(memory_space=pltpu.VMEM), anywhere, anywhere),
        scratch_shapes=[
            pltpu.VMEM((UD, D), F32),
            pltpu.VMEM((ID, D), F32),
            pltpu.VMEM((UD, D), F32),
            pltpu.VMEM((ID, D), F32),
            pltpu.VMEM((1, ID), jnp.int32),
            pltpu.VMEM((1, UD), jnp.int32),
            dma(4),
            pltpu.VMEM((NZ, UD, D), BF16),
            pltpu.VMEM((2, 2 * HALF, D), BF16),
            pltpu.VMEM((2, NY, NX, 1, 128), F32),
            pltpu.VMEM((D, 4 * HALF), BF16),
            pltpu.VMEM((4 * HALF, 128), F32),
            pltpu.VMEM((4 * HALF, NZ * UD), BF16),
            pltpu.VMEM((NB, NZ, D, UD), F32),
            pltpu.VMEM((NB, NZ, UD), F32),
            pltpu.VMEM((NB, NZ, UD), F32),
            pltpu.VMEM((2, 8, 128), F32),
            pltpu.VMEM((NZ, 2, 8, 128), F32),
            pltpu.VMEM((NZ, D, UD), BF16),
            pltpu.VMEM((NZ, D, UD), BF16),
            pltpu.VMEM((NB, 1, NZ * UD), BF16),
            pltpu.VMEM((2 * HALF, D), F32),
            pltpu.VMEM((2, 2 * HALF, D), BF16),
            pltpu.VMEM((2 * HALF, D), BF16),
            pltpu.VMEM((NY, NX, ID, D), BF16),
            pltpu.VMEM((NY, ID, D), BF16),
            pltpu.VMEM((NY, ID, D), BF16),
            pltpu.VMEM((3, 8, 128), F32),
            pltpu.VMEM((11, 8, 128), F32),
            pltpu.VMEM((ID, D), F32),
            pltpu.VMEM((D, UD), F32),
            dma(15), dma(NZ // 2), dma(NY), dma(NY), dma(3), dma(4), dma(NY), dma(9), dma(2),
        ],
        compiler_params=pltpu.CompilerParams(
            collective_id=0, has_side_effects=True, vmem_limit_bytes=64 * 2**20
        ),
        cost_estimate=pl.CostEstimate(
            flops=6 * 1024 * 2048 * D, bytes_accessed=2**19, transcendentals=1024 * 2048
        ),
        name="towers",
    )(users, items, counts.reshape(1, ID), target_indices.reshape(1, UD))
    small = pl.BlockSpec(memory_space=pltpu.VMEM)
    loss, query, cand = pl.pallas_call(
        settle,
        out_shape=results,
        in_specs=[small, anywhere, anywhere],
        out_specs=(small, anywhere, anywhere),
        scratch_shapes=[pltpu.VMEM((UD, D), F32), pltpu.VMEM((ID, D), F32), dma(2), dma(2)],
        compiler_params=pltpu.CompilerParams(vmem_limit_bytes=64 * 2**20),
        name="settle",
    )(*found)
    return loss.reshape(()), query, cand


def solution(mesh):
    placed = P(("blk", "grp"))
    wide = P(("blk", "grp"), None)
    return jax.shard_map(
        on_device,
        mesh=mesh,
        in_specs=(wide, wide, placed, placed),
        out_specs=(P(), wide, wide),
        check_vma=False,
    )
```

```python
import functools
import math

import jax
import jax.numpy as jnp
from jax import lax
from jax.experimental import pallas as pl
from jax.experimental.pallas import tpu as pltpu
from jax.sharding import PartitionSpec as P

scaling_divisor = 5.0
LOG2E = math.log2(math.e)
LN2 = math.log(2.0)
MESH = pl.DeviceIdType.MESH
BF16 = jnp.bfloat16
F32 = jnp.float32

NX, NY, NZ = 4, 8, 8
UD, ID, D = 128, 32, 256
ORDER = (0, 1, 7, 2, 6, 3, 5, 4)
SLOT = tuple(ORDER.index(k) for k in range(NY))
HALF = NX * NY * ID // 2
BLOCKS = tuple((i, r, n) for i in range(2) for r, n in ((0, 512), (512, 256), (768, 256)))
NB = len(BLOCKS)


def dot(a, b, ca=1, cb=0):
    return lax.dot_general(a, b, (((ca,), (cb,)), ((), ())), preferred_element_type=F32)


def kernel(
    users_hbm, items_hbm, counts_hbm, tgt_hbm,
    loss_ref, query_hbm, cand_hbm,
    query_ref, cand_ref,
    users_ref, items_ref, counts_ref, tgt_ref, in_sem,
    rows, it, lq, it_t, lqc, p_all, acc, mst, lst, st_out, st_in, pt_out, pt_in,
    w_row, own_f, ip, xc_in, xs_in, ys_out, ys_in, loss_out, loss_in, tq_s, tv_s,
    sent, z_rs, y_rs, x_rs, c_rs, xc_rs, xs_rs, got, out_sem,
):
    b = lax.axis_index("blk")
    g = lax.axis_index("grp")
    x = (b // 16) * 2 + g % 2
    y = (b // 2) % 8
    z = g // 2
    core = b % 2

    def device(dx=0, dy=0, dz=0, dc=0):
        xx = (x + dx) % NX
        return (
            ((xx // 2) * 8 + (y + dy) % NY) * 2 + (core + dc) % 2,
            ((z + dz) % NZ) * 2 + xx % 2,
        )

    Z_S, Y_S, QL_S, X_S, QX_S, C_S, QC_S, ST_S, PT_S, XC_S, XS_S, YS_S, L0_S, L1_S, L2_S = (
        sent.at[k] for k in range(15)
    )
    QL_R, QX_R, QC_R, ST_R, PT_R, YS_R, L0_R, L1_R, L2_R = (got.at[k] for k in range(9))

    def whole(ref, sem):
        pltpu.make_async_copy(ref, ref, sem).wait()

    def copy(src, dst, ss, rs, **to):
        return pltpu.make_async_remote_copy(
            src_ref=src, dst_ref=dst, send_sem=ss, recv_sem=rs,
            device_id=device(**to), device_id_type=MESH,
        )

    loads = [
        pltpu.make_async_copy(src, dst, in_sem.at[k])
        for k, (src, dst) in enumerate((
            (counts_hbm, counts_ref), (items_hbm, items_ref), (users_hbm, users_ref), (tgt_hbm, tgt_ref)
        ))
    ]
    for load in loads:
        load.start()

    barrier = pltpu.get_barrier_semaphore()
    for d in range(1, NZ):
        pl.semaphore_signal(barrier, inc=1, device_id=device(dz=d), device_id_type=MESH)
    for d in range(1, NY):
        pl.semaphore_signal(barrier, inc=1, device_id=device(dy=d), device_id_type=MESH)
    for d in range(1, NX):
        pl.semaphore_signal(barrier, inc=1, device_id=device(dx=d), device_id_type=MESH)
    pl.semaphore_signal(barrier, inc=1, device_id=device(dc=1), device_id_type=MESH)

    loads[0].wait()
    loads[1].wait()
    it[0, 0:ID, :] = items_ref[...].astype(BF16)
    logq = jnp.log(counts_ref[...].astype(F32)).astype(BF16).astype(F32)
    logq = jnp.concatenate([logq, jnp.zeros((1, 128 - ID), F32)], axis=1)
    lq[0, 0, 0] = logq

    pl.semaphore_wait(barrier, NZ + NY + NX - 3 + 1)

    def z_copy(d, origin=0, part=slice(0, UD)):
        s = SLOT[(NZ + origin - d) % NZ]
        src = rows.at[SLOT[origin], part]
        return copy(src, rows.at[s, part], Z_S, z_rs.at[s], dz=d)

    def z_forward():
        for origin, near, far, part in (
            (6, 1, 2, slice(0, UD // 2)),
            (2, 7, 6, slice(UD // 2, UD)),
        ):
            whole(rows.at[SLOT[origin]], z_rs.at[SLOT[origin]])
            z_copy(far, origin, part).start()
            z_copy(near, origin).start()

    def y_copy(d):
        s = SLOT[(NY - d) % NY]
        return copy(
            it.at[0, pl.ds(0, ID)], it.at[0, pl.ds(s * NX * ID, ID)], Y_S, y_rs.at[s], dy=d
        )

    def ql_copy(d):
        s = SLOT[(NY - d) % NY]
        return copy(lq.at[0, 0, 0], lq.at[0, s, 0], QL_S, QL_R, dy=d)

    def x_copy(s, e):
        return copy(
            it.at[0, pl.ds(s * NX * ID, ID)],
            it.at[0, pl.ds((s * NX + NX - e) * ID, ID)],
            X_S, x_rs.at[s], dx=e,
        )

    def qx_copy(e):
        return copy(lq.at[0, :, 0], lq.at[0, :, NX - e], QX_S, QX_R, dx=e)

    def c_copy(s):
        part = pl.ds(s * NX * ID, NX * ID)
        return copy(it.at[0, part], it.at[1, part], C_S, c_rs.at[max(s // 2 - 1, 0)], dc=1)

    def qc_copy():
        return copy(lq.at[0], lq.at[1], QC_S, QC_R, dc=1)

    for d in (4, 1, 7, 3, 5, 2, 6):
        y_copy(d).start()
    for d in (4, 1, 7, 3, 5, 2, 6):
        ql_copy(d).start()
    for e in range(1, NX):
        x_copy(0, e).start()
    loads[2].wait()
    rows[0] = users_ref[...].astype(BF16)
    for d in (2, 6, 1, 7):
        z_copy(d).start()

    def forward(s):
        whole(it.at[0, pl.ds(s * NX * ID, ID)], y_rs.at[s])
        for e in range(1, NX):
            x_copy(s, e).start()

    for s in range(1, 4):
        forward(s)
    whole(lq.at[0, 1:NY, 0], QL_R)
    for e in range(1, NX):
        qx_copy(e).start()
    for s in range(4, 8):
        forward(s)
    z_forward()

    first = (b * 16 + g) * ID
    loads[3].wait()
    hot = (
        lax.broadcasted_iota(jnp.int32, (ID, UD), 0) + first == tgt_ref[...]
    ).astype(F32)
    hot_half = hot.astype(BF16)
    own_items = it[0, 0:ID, :]
    tq = dot(hot_half, rows[0])
    tq_s[...] = tq
    tv_s[...] = dot(own_items, hot_half, 0, 0)
    eye = (
        lax.broadcasted_iota(jnp.int32, (ID, 128), 0)
        == lax.broadcasted_iota(jnp.int32, (ID, 128), 1)
    )
    own_logq = jnp.where(eye, jnp.broadcast_to(logq, (ID, 128)), 0.0)
    named = jnp.sum(hot, axis=1, keepdims=True)
    pos = jnp.sum(
        jnp.sum(tq * own_items.astype(F32), axis=1, keepdims=True) * (1.0 / scaling_divisor)
        - jnp.sum(own_logq, axis=1, keepdims=True) * named,
        axis=0, keepdims=True,
    )
    st_out[1] = jnp.broadcast_to(pos, (8, 128))

    def arrived(s):
        whole(it.at[0, pl.ds((s * NX + 1) * ID, 3 * ID)], x_rs.at[s])
        c_copy(s).start()

    ones = jnp.ones((128, 128), BF16)

    def spot_of(blk):
        side, row, n = BLOCKS[blk]
        return slice(side * 2 * HALF + row, side * 2 * HALF + row + n)

    def prepare(blk):
        side, row, n = BLOCKS[blk]
        it_t[:, spot_of(blk)] = it[side, row : row + n, :].T
        shards = n // ID
        first_slot = row // (NX * ID)
        found = lq[side, first_slot : first_slot + shards // NX].reshape(shards, 1, 128)
        spread = jnp.where(eye[None], jnp.broadcast_to(found, (shards, ID, 128)), 0.0)
        lqc[spot_of(blk), :] = dot(spread.reshape(n, 128).astype(BF16), ones) * LOG2E

    def unit(blk, k):
        side, row, n = BLOCKS[blk]
        pair = rows[2 * k : 2 * k + 2].reshape(2 * UD, D)
        scores = dot(it[side, row : row + n, :], pair, 1, 1)
        lift = lqc[spot_of(blk), :]
        t = scores * (LOG2E / scaling_divisor) - jnp.concatenate([lift, lift], axis=1)
        m = jnp.max(t, axis=0, keepdims=True)
        p = jnp.exp2(t - m)
        total = jnp.sum(p, axis=0, keepdims=True)
        p_all[spot_of(blk), 2 * k * UD : 2 * (k + 1) * UD] = p.astype(BF16)
        for i in range(2):
            s, lanes = ORDER[2 * k + i], slice(i * UD, (i + 1) * UD)
            mst[blk, s : s + 1, :] = m[:, lanes]
            lst[blk, s : s + 1, :] = total[:, lanes]

    def weighted(blk, k):
        part = dot(it_t[:, spot_of(blk)], p_all[spot_of(blk), 2 * k * UD : 2 * (k + 1) * UD])
        for i in range(2):
            acc[blk, ORDER[2 * k + i]] = part[:, i * UD : (i + 1) * UD]

    def wait_users(k):
        for s in ((1,), (2,), (5,), (6, 7))[k]:
            whole(rows.at[s], z_rs.at[s])

    def wait_other(k):
        row, n = ((0, 512), (512, 256), (768, 256))[k]
        whole(it.at[1, pl.ds(row, n)], c_rs.at[k])

    for s in range(4):
        arrived(s)
    whole(lq.at[0, :, 1:NX], QX_R)
    qc_copy().start()
    prepare(0)
    wait_users(0)
    wait_users(1)
    unit(0, 0)
    unit(0, 1)
    arrived(4)
    arrived(5)
    qc_copy().wait_recv()
    wait_other(0)
    prepare(1)
    prepare(3)
    for blk in (1, 3):
        unit(blk, 0)
        unit(blk, 1)
    arrived(6)
    arrived(7)
    prepare(2)
    unit(2, 0)
    unit(2, 1)
    for k in (2, 3):
        wait_users(k)
        for blk in range(4):
            unit(blk, k)
    for blk in (4, 5):
        wait_other(blk - 3)
        prepare(blk)
        for k in range(4):
            unit(blk, k)

    top = jnp.max(mst[...], axis=0)
    local = top + jnp.log2(sum(lst[k] * jnp.exp2(mst[k] - top) for k in range(NB)))
    st_out[0] = local

    def st_copy(d):
        return copy(st_out, st_in.at[(NZ - d) % NZ], ST_S, ST_R, dz=d)

    def pt_copy(d):
        return copy(pt_out.at[d], pt_in.at[(NZ - d) % NZ], PT_S, PT_R, dz=d)

    for d in (4, 3, 5, 2, 6, 1, 7):
        st_copy(d).start()

    for k in range(NB):
        lst[k] = jnp.exp2(mst[k] - local)
    for k in (3, 2, 1, 0):
        for blk in range(NB):
            weighted(blk, k)

    def part_of(s):
        return sum(acc[k, s] * lst[k, pl.ds(s, 1), :] for k in range(NB))

    def give(s, carry):
        pt_out[s] = part_of(s).astype(BF16)
        pt_copy(s).start()
        return carry

    lax.fori_loop(1, NZ, give, 0)

    whole(rows.at[1:NZ], Z_S)
    whole(it.at[0, pl.ds(0, 7 * ID)], Y_S)
    whole(lq.at[0, 1:NY, 0], QL_S)
    whole(it.at[0, pl.ds(0, 24 * ID)], X_S)
    whole(lq.at[0, :, 1:NX], QX_S)
    whole(it.at[0], C_S)
    whole(lq.at[0], QC_S)

    whole(st_in.at[1:NZ], ST_R)
    seen = [local] + [jnp.roll(st_in[e, 0], e, axis=0) for e in range(1, NZ)]
    top = functools.reduce(jnp.maximum, seen)
    lse = top + jnp.log2(sum(jnp.exp2(v - top) for v in seen))
    share = [jnp.exp2(v[0:1] - lse[0:1]) for v in seen]
    for k in range(NB):
        w = jnp.exp2(mst[k] - lse).astype(BF16)
        for i, s in enumerate(ORDER):
            w_row[k, :, i * UD : (i + 1) * UD] = w[s : s + 1, :]

    users_all = rows[...].reshape(NZ * UD, D)

    def item_part(blk, row, n):
        return dot(p_all[row : row + n, :] * w_row[blk], users_all)

    QUARTER = HALF // 2

    def xc_copy(c):
        part = pl.ds(c * QUARTER, QUARTER)
        return copy(ip.at[1, part], xc_in.at[part], XC_S, xc_rs.at[c], dc=1)

    for c, blk in ((3, 5), (2, 4), (1, 3), (0, 3)):
        part = item_part(blk, 2 * HALF + c * QUARTER, QUARTER)
        ip[1, c * QUARTER : (c + 1) * QUARTER, :] = part.astype(BF16)
        xc_copy(c).start()
    for blk in (2, 1, 0):
        own_f[spot_of(blk), :] = item_part(blk, BLOCKS[blk][1], BLOCKS[blk][2])

    def ls_copy(i, j, **to):
        ss, rs = ((L0_S, L0_R), (L1_S, L1_R), (L2_S, L2_R))[i]
        return copy(loss_out.at[i], loss_in.at[j], ss, rs, **to)

    pos_all = st_out[1] + sum(st_in[e, 1] for e in range(1, NZ))
    line = jnp.sum(jnp.sum(lse, axis=1, keepdims=True), axis=0, keepdims=True) * LN2
    loss_out[0] = jnp.broadcast_to(line, (8, 128)) - pos_all
    ls_copy(0, 0, dc=1).start()

    def xs_copy(s, e):
        return copy(
            ip.at[0, pl.ds((s * NX + e) * ID, ID)], xs_in.at[s, NX - e],
            XS_S, xs_rs.at[s], dx=e,
        )

    for c in (3, 2, 1, 0):
        xc_copy(c).wait_recv()
        for k in (2 * c + 1, 2 * c):
            spot = slice(k * NX * ID, (k + 1) * NX * ID)
            total = own_f[spot, :] + xc_in[spot, :].astype(F32)
            own_f[spot, :] = total
            ip[0, spot, :] = total.astype(BF16)
            for e in (2, 1, 3):
                xs_copy(k, e).start()

    whole(loss_in.at[0], L0_R)
    loss_out[1] = loss_out[0] + loss_in[0]
    for e in range(1, NX):
        ls_copy(1, e, dx=e).start()

    def ys_copy(s):
        mirror = SLOT[(NY - ORDER[s]) % NY]
        return copy(
            ys_out.at[s], ys_in.at[mirror], YS_S, YS_R, dy=ORDER[s]
        )

    def x_total(s):
        whole(xs_in.at[s, 1:NX], xs_rs.at[s])
        spot = slice(s * NX * ID, s * NX * ID + ID)
        return own_f[spot, :] + sum(xs_in[s, e].astype(F32) for e in range(1, NX))

    for s in range(NY - 1, 0, -1):
        ys_out[s] = x_total(s).astype(BF16)
        ys_copy(s).start()
    whole(loss_in.at[1:NX], L1_R)
    loss_out[2] = loss_out[1] + loss_in[1] + loss_in[2] + loss_in[3]
    for d in range(1, NY):
        ls_copy(2, 3 + d, dy=d).start()
    cand = x_total(0) - tq_s[...]

    user_sum = part_of(0) * share[0] - tv_s[...]
    whole(pt_in.at[1:NZ], PT_R)
    for e in range(1, NZ):
        user_sum = user_sum + pt_in[e].astype(F32) * share[e]
    query_ref[...] = user_sum.T * (1.0 / scaling_divisor)
    query_out = pltpu.make_async_copy(query_ref, query_hbm, out_sem.at[0])
    query_out.start()
    whole(st_in.at[1:NZ], ST_S)
    whole(pt_in.at[1:NZ], PT_S)
    whole(ip.at[1], XC_S)
    whole(xs_in.at[:, 1:NX], XS_S)
    whole(loss_in.at[0], L0_S)
    whole(loss_in.at[1:NX], L1_S)

    whole(ys_in.at[1:NY], YS_R)
    for s in range(1, NY):
        cand = cand + ys_in[s].astype(F32)
    cand_ref[...] = cand * (1.0 / scaling_divisor)
    cand_out = pltpu.make_async_copy(cand_ref, cand_hbm, out_sem.at[1])
    cand_out.start()
    total = loss_out[2]
    whole(loss_in.at[4:11], L2_R)
    for d in range(1, NY):
        total = total + loss_in[3 + d]
    loss_ref[...] = total[0:1, 0:1] * (1.0 / (2 * NX * NY * NZ * UD))

    whole(ys_in.at[1:NY], YS_S)
    whole(loss_in.at[4:11], L2_S)
    query_out.wait()
    cand_out.wait()


def settle(
    loss_in, query_in, cand_in, loss_out, query_out, cand_out, query_v, cand_v, in_sem, out_sem
):
    ins = [
        pltpu.make_async_copy(query_in, query_v, in_sem.at[0]),
        pltpu.make_async_copy(cand_in, cand_v, in_sem.at[1]),
    ]
    outs = [
        pltpu.make_async_copy(query_v, query_out, out_sem.at[0]),
        pltpu.make_async_copy(cand_v, cand_out, out_sem.at[1]),
    ]
    for move in ins:
        move.start()
    loss_out[...] = loss_in[...]
    for arrival, departure in zip(ins, outs):
        arrival.wait()
        departure.start()
    for departure in outs:
        departure.wait()


def on_device(users, items, counts, target_indices):
    dma = lambda *n: pltpu.SemaphoreType.DMA(n)
    anywhere = pl.BlockSpec(memory_space=pl.ANY)
    results = (
        jax.ShapeDtypeStruct((1, 1), F32),
        jax.ShapeDtypeStruct((UD, D), F32),
        jax.ShapeDtypeStruct((ID, D), F32),
    )
    found = pl.pallas_call(
        kernel,
        out_shape=results,
        in_specs=[anywhere] * 4,
        out_specs=(pl.BlockSpec(memory_space=pltpu.VMEM), anywhere, anywhere),
        scratch_shapes=[
            pltpu.VMEM((UD, D), F32),
            pltpu.VMEM((ID, D), F32),
            pltpu.VMEM((UD, D), F32),
            pltpu.VMEM((ID, D), F32),
            pltpu.VMEM((1, ID), jnp.int32),
            pltpu.VMEM((1, UD), jnp.int32),
            dma(4),
            pltpu.VMEM((NZ, UD, D), BF16),
            pltpu.VMEM((2, 2 * HALF, D), BF16),
            pltpu.VMEM((2, NY, NX, 1, 128), F32),
            pltpu.VMEM((D, 4 * HALF), BF16),
            pltpu.VMEM((4 * HALF, 128), F32),
            pltpu.VMEM((4 * HALF, NZ * UD), BF16),
            pltpu.VMEM((NB, NZ, D, UD), F32),
            pltpu.VMEM((NB, NZ, UD), F32),
            pltpu.VMEM((NB, NZ, UD), F32),
            pltpu.VMEM((2, 8, 128), F32),
            pltpu.VMEM((NZ, 2, 8, 128), F32),
            pltpu.VMEM((NZ, D, UD), BF16),
            pltpu.VMEM((NZ, D, UD), BF16),
            pltpu.VMEM((NB, 1, NZ * UD), BF16),
            pltpu.VMEM((2 * HALF, D), F32),
            pltpu.VMEM((2, 2 * HALF, D), BF16),
            pltpu.VMEM((2 * HALF, D), BF16),
            pltpu.VMEM((NY, NX, ID, D), BF16),
            pltpu.VMEM((NY, ID, D), BF16),
            pltpu.VMEM((NY, ID, D), BF16),
            pltpu.VMEM((3, 8, 128), F32),
            pltpu.VMEM((11, 8, 128), F32),
            pltpu.VMEM((ID, D), F32),
            pltpu.VMEM((D, UD), F32),
            dma(15), dma(NZ), dma(NY), dma(NY), dma(3), dma(4), dma(NY), dma(9), dma(2),
        ],
        compiler_params=pltpu.CompilerParams(
            collective_id=0, has_side_effects=True, vmem_limit_bytes=64 * 2**20
        ),
        cost_estimate=pl.CostEstimate(
            flops=6 * 1024 * 2048 * D, bytes_accessed=2**19, transcendentals=1024 * 2048
        ),
        name="towers",
    )(users, items, counts.reshape(1, ID), target_indices.reshape(1, UD))
    small = pl.BlockSpec(memory_space=pltpu.VMEM)
    loss, query, cand = pl.pallas_call(
        settle,
        out_shape=results,
        in_specs=[small, anywhere, anywhere],
        out_specs=(small, anywhere, anywhere),
        scratch_shapes=[pltpu.VMEM((UD, D), F32), pltpu.VMEM((ID, D), F32), dma(2), dma(2)],
        compiler_params=pltpu.CompilerParams(vmem_limit_bytes=64 * 2**20),
        name="settle",
    )(*found)
    return loss.reshape(()), query, cand


def solution(mesh):
    placed = P(("blk", "grp"))
    wide = P(("blk", "grp"), None)
    return jax.shard_map(
        on_device,
        mesh=mesh,
        in_specs=(wide, wide, placed, placed),
        out_specs=(P(), wide, wide),
        check_vma=False,
    )
```

```python
import functools
import math

import jax
import jax.numpy as jnp
from jax import lax
from jax.experimental import pallas as pl
from jax.experimental.pallas import tpu as pltpu
from jax.sharding import PartitionSpec as P

scaling_divisor = 5.0
LOG2E = math.log2(math.e)
LN2 = math.log(2.0)
MESH = pl.DeviceIdType.MESH
BF16 = jnp.bfloat16
F32 = jnp.float32

NX, NY, NZ = 4, 8, 8
UD, ID, D = 128, 32, 256
ORDER = (0, 1, 7, 2, 6, 3, 5, 4)
SLOT = tuple(ORDER.index(k) for k in range(NY))
HALF = NX * NY * ID // 2
BLOCKS = tuple((i, r, n) for i in range(2) for r, n in ((0, 512), (512, 256), (768, 256)))
NB = len(BLOCKS)


def dot(a, b, ca=1, cb=0):
    return lax.dot_general(a, b, (((ca,), (cb,)), ((), ())), preferred_element_type=F32)


def kernel(
    users_hbm, items_hbm, counts_hbm, tgt_hbm,
    loss_hbm, query_hbm, cand_hbm,
    loss_ref, query_ref, cand_ref,
    users_ref, items_ref, counts_ref, tgt_ref, in_sem,
    rows, it, lq, it_t, lqc, p_all, acc, mst, lst, st_out, st_in, pt_out, pt_in,
    w_row, own_f, ip, xc_in, xs_in, ys_out, ys_in, loss_out, loss_in, tq_s, tv_s,
    sent, z_rs, y_rs, x_rs, c_rs, xc_rs, xs_rs, got, out_sem,
):
    b = lax.axis_index("blk")
    g = lax.axis_index("grp")
    x = (b // 16) * 2 + g % 2
    y = (b // 2) % 8
    z = g // 2
    core = b % 2

    def device(dx=0, dy=0, dz=0, dc=0):
        xx = (x + dx) % NX
        return (
            ((xx // 2) * 8 + (y + dy) % NY) * 2 + (core + dc) % 2,
            ((z + dz) % NZ) * 2 + xx % 2,
        )

    Z_S, Y_S, QL_S, X_S, QX_S, C_S, QC_S, ST_S, PT_S, XC_S, XS_S, YS_S, L0_S, L1_S, L2_S = (
        sent.at[k] for k in range(15)
    )
    QL_R, QX_R, QC_R, ST_R, PT_R, YS_R, L0_R, L1_R, L2_R = (got.at[k] for k in range(9))

    def whole(ref, sem):
        pltpu.make_async_copy(ref, ref, sem).wait()

    def copy(src, dst, ss, rs, **to):
        return pltpu.make_async_remote_copy(
            src_ref=src, dst_ref=dst, send_sem=ss, recv_sem=rs,
            device_id=device(**to), device_id_type=MESH,
        )

    loads = [
        pltpu.make_async_copy(src, dst, in_sem.at[k])
        for k, (src, dst) in enumerate((
            (counts_hbm, counts_ref), (items_hbm, items_ref), (users_hbm, users_ref), (tgt_hbm, tgt_ref)
        ))
    ]
    for load in loads:
        load.start()

    barrier = pltpu.get_barrier_semaphore()
    for d in range(1, NZ):
        pl.semaphore_signal(barrier, inc=1, device_id=device(dz=d), device_id_type=MESH)
    for d in range(1, NY):
        pl.semaphore_signal(barrier, inc=1, device_id=device(dy=d), device_id_type=MESH)
    for d in range(1, NX):
        pl.semaphore_signal(barrier, inc=1, device_id=device(dx=d), device_id_type=MESH)
    pl.semaphore_signal(barrier, inc=1, device_id=device(dc=1), device_id_type=MESH)

    loads[0].wait()
    loads[1].wait()
    it[0, 0:ID, :] = items_ref[...].astype(BF16)
    logq = jnp.log(counts_ref[...].astype(F32)).astype(BF16).astype(F32)
    logq = jnp.concatenate([logq, jnp.zeros((1, 128 - ID), F32)], axis=1)
    lq[0, 0, 0] = logq

    pl.semaphore_wait(barrier, NZ + NY + NX - 3 + 1)

    def z_copy(d, origin=0, part=slice(0, UD)):
        s = SLOT[(NZ + origin - d) % NZ]
        src = rows.at[SLOT[origin], part]
        return copy(src, rows.at[s, part], Z_S, z_rs.at[s], dz=d)

    def z_forward():
        for origin, near, far, part in (
            (6, 1, 2, slice(0, UD // 2)),
            (2, 7, 6, slice(UD // 2, UD)),
        ):
            whole(rows.at[SLOT[origin]], z_rs.at[SLOT[origin]])
            z_copy(far, origin, part).start()
            z_copy(near, origin).start()

    def y_copy(d):
        s = SLOT[(NY - d) % NY]
        return copy(
            it.at[0, pl.ds(0, ID)], it.at[0, pl.ds(s * NX * ID, ID)], Y_S, y_rs.at[s], dy=d
        )

    def ql_copy(d):
        s = SLOT[(NY - d) % NY]
        return copy(lq.at[0, 0, 0], lq.at[0, s, 0], QL_S, QL_R, dy=d)

    def x_copy(s, e):
        return copy(
            it.at[0, pl.ds(s * NX * ID, ID)],
            it.at[0, pl.ds((s * NX + NX - e) * ID, ID)],
            X_S, x_rs.at[s], dx=e,
        )

    def qx_copy(e):
        return copy(lq.at[0, :, 0], lq.at[0, :, NX - e], QX_S, QX_R, dx=e)

    def c_copy(s):
        part = pl.ds(s * NX * ID, NX * ID)
        return copy(it.at[0, part], it.at[1, part], C_S, c_rs.at[max(s // 2 - 1, 0)], dc=1)

    def qc_copy():
        return copy(lq.at[0], lq.at[1], QC_S, QC_R, dc=1)

    for d in (4, 1, 7, 3, 5, 2, 6):
        y_copy(d).start()
    for d in (4, 1, 7, 3, 5, 2, 6):
        ql_copy(d).start()
    for e in range(1, NX):
        x_copy(0, e).start()
    loads[2].wait()
    rows[0] = users_ref[...].astype(BF16)
    for d in (2, 6, 1, 7):
        z_copy(d).start()

    def forward(s):
        whole(it.at[0, pl.ds(s * NX * ID, ID)], y_rs.at[s])
        for e in range(1, NX):
            x_copy(s, e).start()

    for s in range(1, 4):
        forward(s)
    whole(lq.at[0, 1:NY, 0], QL_R)
    for e in range(1, NX):
        qx_copy(e).start()
    for s in range(4, 8):
        forward(s)
    z_forward()

    first = (b * 16 + g) * ID
    loads[3].wait()
    hot = (
        lax.broadcasted_iota(jnp.int32, (ID, UD), 0) + first == tgt_ref[...]
    ).astype(F32)
    hot_half = hot.astype(BF16)
    own_items = it[0, 0:ID, :]
    tq = dot(hot_half, rows[0])
    tq_s[...] = tq
    tv_s[...] = dot(own_items, hot_half, 0, 0)
    eye = (
        lax.broadcasted_iota(jnp.int32, (ID, 128), 0)
        == lax.broadcasted_iota(jnp.int32, (ID, 128), 1)
    )
    own_logq = jnp.where(eye, jnp.broadcast_to(logq, (ID, 128)), 0.0)
    named = jnp.sum(hot, axis=1, keepdims=True)
    pos = jnp.sum(
        jnp.sum(tq * own_items.astype(F32), axis=1, keepdims=True) * (1.0 / scaling_divisor)
        - jnp.sum(own_logq, axis=1, keepdims=True) * named,
        axis=0, keepdims=True,
    )
    st_out[1] = jnp.broadcast_to(pos, (8, 128))

    def arrived(s):
        whole(it.at[0, pl.ds((s * NX + 1) * ID, 3 * ID)], x_rs.at[s])
        c_copy(s).start()

    ones = jnp.ones((128, 128), BF16)

    def spot_of(blk):
        side, row, n = BLOCKS[blk]
        return slice(side * 2 * HALF + row, side * 2 * HALF + row + n)

    def prepare(blk):
        side, row, n = BLOCKS[blk]
        it_t[:, spot_of(blk)] = it[side, row : row + n, :].T
        shards = n // ID
        first_slot = row // (NX * ID)
        found = lq[side, first_slot : first_slot + shards // NX].reshape(shards, 1, 128)
        spread = jnp.where(eye[None], jnp.broadcast_to(found, (shards, ID, 128)), 0.0)
        lqc[spot_of(blk), :] = dot(spread.reshape(n, 128).astype(BF16), ones) * LOG2E

    def unit(blk, k):
        side, row, n = BLOCKS[blk]
        pair = rows[2 * k : 2 * k + 2].reshape(2 * UD, D)
        scores = dot(it[side, row : row + n, :], pair, 1, 1)
        lift = lqc[spot_of(blk), :]
        t = scores * (LOG2E / scaling_divisor) - jnp.concatenate([lift, lift], axis=1)
        m = jnp.max(t, axis=0, keepdims=True)
        p = jnp.exp2(t - m)
        total = jnp.sum(p, axis=0, keepdims=True)
        p_all[spot_of(blk), 2 * k * UD : 2 * (k + 1) * UD] = p.astype(BF16)
        for i in range(2):
            s, lanes = ORDER[2 * k + i], slice(i * UD, (i + 1) * UD)
            mst[blk, s : s + 1, :] = m[:, lanes]
            lst[blk, s : s + 1, :] = total[:, lanes]

    def weighted(blk, k):
        part = dot(it_t[:, spot_of(blk)], p_all[spot_of(blk), 2 * k * UD : 2 * (k + 1) * UD])
        for i in range(2):
            acc[blk, ORDER[2 * k + i]] = part[:, i * UD : (i + 1) * UD]

    def wait_users(k):
        for s in ((1,), (2,), (5,), (6, 7))[k]:
            whole(rows.at[s], z_rs.at[s])

    def wait_other(k):
        row, n = ((0, 512), (512, 256), (768, 256))[k]
        whole(it.at[1, pl.ds(row, n)], c_rs.at[k])

    for s in range(4):
        arrived(s)
    whole(lq.at[0, :, 1:NX], QX_R)
    qc_copy().start()
    prepare(0)
    wait_users(0)
    wait_users(1)
    unit(0, 0)
    unit(0, 1)
    arrived(4)
    arrived(5)
    qc_copy().wait_recv()
    wait_other(0)
    prepare(1)
    prepare(3)
    for blk in (1, 3):
        unit(blk, 0)
        unit(blk, 1)
    arrived(6)
    arrived(7)
    prepare(2)
    unit(2, 0)
    unit(2, 1)
    for k in (2, 3):
        wait_users(k)
        for blk in range(4):
            unit(blk, k)
    for blk in (4, 5):
        wait_other(blk - 3)
        prepare(blk)
        for k in range(4):
            unit(blk, k)

    top = jnp.max(mst[...], axis=0)
    local = top + jnp.log2(sum(lst[k] * jnp.exp2(mst[k] - top) for k in range(NB)))
    st_out[0] = local

    def st_copy(d):
        return copy(st_out, st_in.at[(NZ - d) % NZ], ST_S, ST_R, dz=d)

    def pt_copy(d):
        return copy(pt_out.at[d], pt_in.at[(NZ - d) % NZ], PT_S, PT_R, dz=d)

    for d in (4, 3, 5, 2, 6, 1, 7):
        st_copy(d).start()

    for k in range(NB):
        lst[k] = jnp.exp2(mst[k] - local)
    for k in (3, 2, 1, 0):
        for blk in range(NB):
            weighted(blk, k)

    def part_of(s):
        return sum(acc[k, s] * lst[k, pl.ds(s, 1), :] for k in range(NB))

    def give(s, carry):
        pt_out[s] = part_of(s).astype(BF16)
        pt_copy(s).start()
        return carry

    lax.fori_loop(1, NZ, give, 0)

    whole(rows.at[1:NZ], Z_S)
    whole(it.at[0, pl.ds(0, 7 * ID)], Y_S)
    whole(lq.at[0, 1:NY, 0], QL_S)
    whole(it.at[0, pl.ds(0, 24 * ID)], X_S)
    whole(lq.at[0, :, 1:NX], QX_S)
    whole(it.at[0], C_S)
    whole(lq.at[0], QC_S)

    whole(st_in.at[1:NZ], ST_R)
    seen = [local] + [jnp.roll(st_in[e, 0], e, axis=0) for e in range(1, NZ)]
    top = functools.reduce(jnp.maximum, seen)
    lse = top + jnp.log2(sum(jnp.exp2(v - top) for v in seen))
    share = [jnp.exp2(v[0:1] - lse[0:1]) for v in seen]
    for k in range(NB):
        w = jnp.exp2(mst[k] - lse).astype(BF16)
        for i, s in enumerate(ORDER):
            w_row[k, :, i * UD : (i + 1) * UD] = w[s : s + 1, :]

    users_all = rows[...].reshape(NZ * UD, D)

    def item_part(blk, row, n):
        return dot(p_all[row : row + n, :] * w_row[blk], users_all)

    QUARTER = HALF // 2

    def xc_copy(c):
        part = pl.ds(c * QUARTER, QUARTER)
        return copy(ip.at[1, part], xc_in.at[part], XC_S, xc_rs.at[c], dc=1)

    for c, blk in ((3, 5), (2, 4), (1, 3), (0, 3)):
        part = item_part(blk, 2 * HALF + c * QUARTER, QUARTER)
        ip[1, c * QUARTER : (c + 1) * QUARTER, :] = part.astype(BF16)
        xc_copy(c).start()
    for blk in (2, 1, 0):
        own_f[spot_of(blk), :] = item_part(blk, BLOCKS[blk][1], BLOCKS[blk][2])

    def ls_copy(i, j, **to):
        ss, rs = ((L0_S, L0_R), (L1_S, L1_R), (L2_S, L2_R))[i]
        return copy(loss_out.at[i], loss_in.at[j], ss, rs, **to)

    pos_all = st_out[1] + sum(st_in[e, 1] for e in range(1, NZ))
    line = jnp.sum(jnp.sum(lse, axis=1, keepdims=True), axis=0, keepdims=True) * LN2
    loss_out[0] = jnp.broadcast_to(line, (8, 128)) - pos_all
    ls_copy(0, 0, dc=1).start()

    def xs_copy(s, e):
        return copy(
            ip.at[0, pl.ds((s * NX + e) * ID, ID)], xs_in.at[s, NX - e],
            XS_S, xs_rs.at[s], dx=e,
        )

    for c in (3, 2, 1, 0):
        xc_copy(c).wait_recv()
        if c == 3:
            whole(loss_in.at[0], L0_R)
            loss_out[1] = loss_out[0] + loss_in[0]
            for e in range(1, NX):
                ls_copy(1, e, dx=e).start()
        for k in (2 * c + 1, 2 * c):
            spot = slice(k * NX * ID, (k + 1) * NX * ID)
            total = own_f[spot, :] + xc_in[spot, :].astype(F32)
            own_f[spot, :] = total
            ip[0, spot, :] = total.astype(BF16)
            for e in (2, 1, 3):
                xs_copy(k, e).start()


    def ys_copy(s):
        mirror = SLOT[(NY - ORDER[s]) % NY]
        return copy(
            ys_out.at[s], ys_in.at[mirror], YS_S, YS_R, dy=ORDER[s]
        )

    def x_total(s):
        whole(xs_in.at[s, 1:NX], xs_rs.at[s])
        spot = slice(s * NX * ID, s * NX * ID + ID)
        return own_f[spot, :] + sum(xs_in[s, e].astype(F32) for e in range(1, NX))

    for s in range(NY - 1, 0, -1):
        ys_out[s] = x_total(s).astype(BF16)
        ys_copy(s).start()
        if s == 6:
            whole(loss_in.at[1:NX], L1_R)
            loss_out[2] = loss_out[1] + loss_in[1] + loss_in[2] + loss_in[3]
            for d in (4, 3, 5, 2, 6, 1, 7):
                ls_copy(2, 3 + d, dy=d).start()
    cand = x_total(0) - tq_s[...]

    user_sum = part_of(0) * share[0] - tv_s[...]
    whole(pt_in.at[1:NZ], PT_R)
    for e in range(1, NZ):
        user_sum = user_sum + pt_in[e].astype(F32) * share[e]
    query_ref[...] = user_sum.T * (1.0 / scaling_divisor)
    query_out = pltpu.make_async_copy(query_ref, query_hbm, out_sem.at[0])
    query_out.start()
    whole(st_in.at[1:NZ], ST_S)
    whole(pt_in.at[1:NZ], PT_S)
    whole(ip.at[1], XC_S)
    whole(xs_in.at[:, 1:NX], XS_S)
    whole(loss_in.at[0], L0_S)
    whole(loss_in.at[1:NX], L1_S)

    whole(ys_in.at[1:NY], YS_R)
    for s in range(1, NY):
        cand = cand + ys_in[s].astype(F32)
    cand_ref[...] = cand * (1.0 / scaling_divisor)
    cand_out = pltpu.make_async_copy(cand_ref, cand_hbm, out_sem.at[1])
    cand_out.start()
    total = loss_out[2]
    whole(loss_in.at[4:11], L2_R)
    for d in range(1, NY):
        total = total + loss_in[3 + d]
    loss_ref[...] = total[0:1, 0:1] * (1.0 / (2 * NX * NY * NZ * UD))
    loss_left = pltpu.make_async_copy(loss_ref, loss_hbm, out_sem.at[2])
    loss_left.start()

    whole(ys_in.at[1:NY], YS_S)
    whole(loss_in.at[4:11], L2_S)
    query_out.wait()
    cand_out.wait()
    loss_left.wait()


def settle(
    loss_in, query_in, cand_in, loss_out, query_out, cand_out,
    loss_v, query_v, cand_v, in_sem, out_sem,
):
    way = (
        (query_in, query_v, query_out), (cand_in, cand_v, cand_out), (loss_in, loss_v, loss_out)
    )
    ins = [pltpu.make_async_copy(a, v, in_sem.at[k]) for k, (a, v, _) in enumerate(way)]
    outs = [pltpu.make_async_copy(v, b, out_sem.at[k]) for k, (_, v, b) in enumerate(way)]
    for move in ins:
        move.start()
    for arrival, departure in zip(ins, outs):
        arrival.wait()
        departure.start()
    for departure in outs:
        departure.wait()


def on_device(users, items, counts, target_indices):
    dma = lambda *n: pltpu.SemaphoreType.DMA(n)
    anywhere = pl.BlockSpec(memory_space=pl.ANY)
    results = (
        jax.ShapeDtypeStruct((1, 1), F32),
        jax.ShapeDtypeStruct((UD, D), F32),
        jax.ShapeDtypeStruct((ID, D), F32),
    )
    found = pl.pallas_call(
        kernel,
        out_shape=results,
        in_specs=[anywhere] * 4,
        out_specs=(anywhere,) * 3,
        scratch_shapes=[
            pltpu.VMEM((1, 1), F32),
            pltpu.VMEM((UD, D), F32),
            pltpu.VMEM((ID, D), F32),
            pltpu.VMEM((UD, D), F32),
            pltpu.VMEM((ID, D), F32),
            pltpu.VMEM((1, ID), jnp.int32),
            pltpu.VMEM((1, UD), jnp.int32),
            dma(4),
            pltpu.VMEM((NZ, UD, D), BF16),
            pltpu.VMEM((2, 2 * HALF, D), BF16),
            pltpu.VMEM((2, NY, NX, 1, 128), F32),
            pltpu.VMEM((D, 4 * HALF), BF16),
            pltpu.VMEM((4 * HALF, 128), F32),
            pltpu.VMEM((4 * HALF, NZ * UD), BF16),
            pltpu.VMEM((NB, NZ, D, UD), F32),
            pltpu.VMEM((NB, NZ, UD), F32),
            pltpu.VMEM((NB, NZ, UD), F32),
            pltpu.VMEM((2, 8, 128), F32),
            pltpu.VMEM((NZ, 2, 8, 128), F32),
            pltpu.VMEM((NZ, D, UD), BF16),
            pltpu.VMEM((NZ, D, UD), BF16),
            pltpu.VMEM((NB, 1, NZ * UD), BF16),
            pltpu.VMEM((2 * HALF, D), F32),
            pltpu.VMEM((2, 2 * HALF, D), BF16),
            pltpu.VMEM((2 * HALF, D), BF16),
            pltpu.VMEM((NY, NX, ID, D), BF16),
            pltpu.VMEM((NY, ID, D), BF16),
            pltpu.VMEM((NY, ID, D), BF16),
            pltpu.VMEM((3, 8, 128), F32),
            pltpu.VMEM((11, 8, 128), F32),
            pltpu.VMEM((ID, D), F32),
            pltpu.VMEM((D, UD), F32),
            dma(15), dma(NZ), dma(NY), dma(NY), dma(3), dma(4), dma(NY), dma(9), dma(3),
        ],
        compiler_params=pltpu.CompilerParams(
            collective_id=0, has_side_effects=True, vmem_limit_bytes=64 * 2**20
        ),
        cost_estimate=pl.CostEstimate(
            flops=6 * 1024 * 2048 * D, bytes_accessed=2**19, transcendentals=1024 * 2048
        ),
        name="towers",
    )(users, items, counts.reshape(1, ID), target_indices.reshape(1, UD))
    loss, query, cand = pl.pallas_call(
        settle,
        out_shape=results,
        in_specs=[anywhere] * 3,
        out_specs=(anywhere,) * 3,
        scratch_shapes=[
            pltpu.VMEM((1, 1), F32), pltpu.VMEM((UD, D), F32), pltpu.VMEM((ID, D), F32), dma(3), dma(3)
        ],
        compiler_params=pltpu.CompilerParams(vmem_limit_bytes=64 * 2**20),
        name="settle",
    )(*found)
    return loss.reshape(()), query, cand


def solution(mesh):
    placed = P(("blk", "grp"))
    wide = P(("blk", "grp"), None)
    return jax.shard_map(
        on_device,
        mesh=mesh,
        in_specs=(wide, wide, placed, placed),
        out_specs=(P(), wide, wide),
        check_vma=False,
    )
```

```python
import functools
import math

import jax
import jax.numpy as jnp
from jax import lax
from jax.experimental import pallas as pl
from jax.experimental.pallas import tpu as pltpu
from jax.sharding import PartitionSpec as P

scaling_divisor = 5.0
LOG2E = math.log2(math.e)
LN2 = math.log(2.0)
MESH = pl.DeviceIdType.MESH
BF16 = jnp.bfloat16
F32 = jnp.float32

NX, NY, NZ = 4, 8, 8
UD, ID, D = 128, 32, 256
ORDER = (0, 1, 7, 2, 6, 3, 5, 4)
SLOT = tuple(ORDER.index(k) for k in range(NY))
HALF = NX * NY * ID // 2
BLOCKS = tuple((i, r, n) for i in range(2) for r, n in ((0, 512), (512, 256), (768, 256)))
NB = len(BLOCKS)


def dot(a, b, ca=1, cb=0):
    return lax.dot_general(a, b, (((ca,), (cb,)), ((), ())), preferred_element_type=F32)


def kernel(
    users_hbm, items_hbm, counts_hbm, tgt_hbm,
    loss_hbm, query_hbm, cand_hbm,
    loss_ref, query_ref, cand_ref,
    users_ref, items_ref, counts_ref, tgt_ref, in_sem,
    rows, it, lq, it_t, lqc, p_all, acc, mst, lst, st_out, st_in, pt_out, pt_in,
    w_row, own_f, ip, xc_in, xs_in, ys_out, ys_in, loss_out, loss_in, tq_s, tv_s,
    sent, z_rs, y_rs, x_rs, c_rs, xc_rs, xs_rs, got, out_sem,
):
    b = lax.axis_index("blk")
    g = lax.axis_index("grp")
    x = (b // 16) * 2 + g % 2
    y = (b // 2) % 8
    z = g // 2
    core = b % 2

    def device(dx=0, dy=0, dz=0, dc=0):
        xx = (x + dx) % NX
        return (
            ((xx // 2) * 8 + (y + dy) % NY) * 2 + (core + dc) % 2,
            ((z + dz) % NZ) * 2 + xx % 2,
        )

    Z_S, Y_S, QL_S, X_S, QX_S, C_S, QC_S, ST_S, PT_S, XC_S, XS_S, YS_S, L0_S, L1_S, L2_S = (
        sent.at[k] for k in range(15)
    )
    QL_R, QX_R, QC_R, ST_R, PT_R, YS_R, L0_R, L1_R, L2_R = (got.at[k] for k in range(9))

    def whole(ref, sem):
        pltpu.make_async_copy(ref, ref, sem).wait()

    def copy(src, dst, ss, rs, **to):
        return pltpu.make_async_remote_copy(
            src_ref=src, dst_ref=dst, send_sem=ss, recv_sem=rs,
            device_id=device(**to), device_id_type=MESH,
        )

    loads = [
        pltpu.make_async_copy(src, dst, in_sem.at[k])
        for k, (src, dst) in enumerate((
            (counts_hbm, counts_ref), (items_hbm, items_ref), (users_hbm, users_ref), (tgt_hbm, tgt_ref)
        ))
    ]
    for load in loads:
        load.start()

    barrier = pltpu.get_barrier_semaphore()
    for d in (4, 3, 5, 2, 6, 1, 7):
        pl.semaphore_signal(barrier, inc=1, device_id=device(dz=d), device_id_type=MESH)
    for d in (4, 3, 5, 2, 6, 1, 7):
        pl.semaphore_signal(barrier, inc=1, device_id=device(dy=d), device_id_type=MESH)
    for d in range(1, NX):
        pl.semaphore_signal(barrier, inc=1, device_id=device(dx=d), device_id_type=MESH)
    pl.semaphore_signal(barrier, inc=1, device_id=device(dc=1), device_id_type=MESH)

    loads[0].wait()
    loads[1].wait()
    it[0, 0:ID, :] = items_ref[...].astype(BF16)
    logq = jnp.log(counts_ref[...].astype(F32)).astype(BF16).astype(F32)
    logq = jnp.concatenate([logq, jnp.zeros((1, 128 - ID), F32)], axis=1)
    lq[0, 0, 0] = logq

    pl.semaphore_wait(barrier, NZ + NY + NX - 3 + 1)

    def z_copy(d, origin=0, part=slice(0, UD)):
        s = SLOT[(NZ + origin - d) % NZ]
        src = rows.at[SLOT[origin], part]
        return copy(src, rows.at[s, part], Z_S, z_rs.at[s], dz=d)

    def z_forward():
        for origin, near, far, part in (
            (6, 1, 2, slice(0, UD // 2)),
            (2, 7, 6, slice(UD // 2, UD)),
        ):
            whole(rows.at[SLOT[origin]], z_rs.at[SLOT[origin]])
            z_copy(far, origin, part).start()
            z_copy(near, origin).start()

    def y_copy(d):
        s = SLOT[(NY - d) % NY]
        return copy(
            it.at[0, pl.ds(0, ID)], it.at[0, pl.ds(s * NX * ID, ID)], Y_S, y_rs.at[s], dy=d
        )

    def ql_copy(d):
        s = SLOT[(NY - d) % NY]
        return copy(lq.at[0, 0, 0], lq.at[0, s, 0], QL_S, QL_R, dy=d)

    def x_copy(s, e):
        return copy(
            it.at[0, pl.ds(s * NX * ID, ID)],
            it.at[0, pl.ds((s * NX + NX - e) * ID, ID)],
            X_S, x_rs.at[s], dx=e,
        )

    def qx_copy(e):
        return copy(lq.at[0, :, 0], lq.at[0, :, NX - e], QX_S, QX_R, dx=e)

    def c_copy(s):
        part = pl.ds(s * NX * ID, NX * ID)
        return copy(it.at[0, part], it.at[1, part], C_S, c_rs.at[max(s // 2 - 1, 0)], dc=1)

    def qc_copy():
        return copy(lq.at[0], lq.at[1], QC_S, QC_R, dc=1)

    for d in (4, 1, 7, 3, 5, 2, 6):
        y_copy(d).start()
    for d in (4, 1, 7, 3, 5, 2, 6):
        ql_copy(d).start()
    for e in range(1, NX):
        x_copy(0, e).start()
    loads[2].wait()
    rows[0] = users_ref[...].astype(BF16)
    for d in (2, 6, 1, 7):
        z_copy(d).start()

    def forward(s):
        whole(it.at[0, pl.ds(s * NX * ID, ID)], y_rs.at[s])
        for e in (2, 1, 3):
            x_copy(s, e).start()

    for s in range(1, 4):
        forward(s)
    whole(lq.at[0, 1:NY, 0], QL_R)
    for e in range(1, NX):
        qx_copy(e).start()
    for s in range(4, 8):
        forward(s)
    z_forward()

    first = (b * 16 + g) * ID
    loads[3].wait()
    hot = (
        lax.broadcasted_iota(jnp.int32, (ID, UD), 0) + first == tgt_ref[...]
    ).astype(F32)
    hot_half = hot.astype(BF16)
    own_items = it[0, 0:ID, :]
    tq = dot(hot_half, rows[0])
    tq_s[...] = tq
    tv_s[...] = dot(own_items, hot_half, 0, 0)
    eye = (
        lax.broadcasted_iota(jnp.int32, (ID, 128), 0)
        == lax.broadcasted_iota(jnp.int32, (ID, 128), 1)
    )
    own_logq = jnp.where(eye, jnp.broadcast_to(logq, (ID, 128)), 0.0)
    named = jnp.sum(hot, axis=1, keepdims=True)
    pos = jnp.sum(
        jnp.sum(tq * own_items.astype(F32), axis=1, keepdims=True) * (1.0 / scaling_divisor)
        - jnp.sum(own_logq, axis=1, keepdims=True) * named,
        axis=0, keepdims=True,
    )
    st_out[1] = jnp.broadcast_to(pos, (8, 128))

    def arrived(s):
        whole(it.at[0, pl.ds((s * NX + 1) * ID, 3 * ID)], x_rs.at[s])
        c_copy(s).start()

    ones = jnp.ones((128, 128), BF16)

    def spot_of(blk):
        side, row, n = BLOCKS[blk]
        return slice(side * 2 * HALF + row, side * 2 * HALF + row + n)

    def prepare(blk):
        side, row, n = BLOCKS[blk]
        it_t[:, spot_of(blk)] = it[side, row : row + n, :].T
        shards = n // ID
        first_slot = row // (NX * ID)
        found = lq[side, first_slot : first_slot + shards // NX].reshape(shards, 1, 128)
        spread = jnp.where(eye[None], jnp.broadcast_to(found, (shards, ID, 128)), 0.0)
        lqc[spot_of(blk), :] = dot(spread.reshape(n, 128).astype(BF16), ones) * LOG2E

    def unit(blk, k):
        side, row, n = BLOCKS[blk]
        pair = rows[2 * k : 2 * k + 2].reshape(2 * UD, D)
        scores = dot(it[side, row : row + n, :], pair, 1, 1)
        lift = lqc[spot_of(blk), :]
        t = scores * (LOG2E / scaling_divisor) - jnp.concatenate([lift, lift], axis=1)
        m = jnp.max(t, axis=0, keepdims=True)
        p = jnp.exp2(t - m)
        total = jnp.sum(p, axis=0, keepdims=True)
        p_all[spot_of(blk), 2 * k * UD : 2 * (k + 1) * UD] = p.astype(BF16)
        for i in range(2):
            s, lanes = ORDER[2 * k + i], slice(i * UD, (i + 1) * UD)
            mst[blk, s : s + 1, :] = m[:, lanes]
            lst[blk, s : s + 1, :] = total[:, lanes]

    def weighted(blk, k):
        part = dot(it_t[:, spot_of(blk)], p_all[spot_of(blk), 2 * k * UD : 2 * (k + 1) * UD])
        for i in range(2):
            acc[blk, ORDER[2 * k + i]] = part[:, i * UD : (i + 1) * UD]

    def wait_users(k):
        for s in ((1,), (2,), (5,), (6, 7))[k]:
            whole(rows.at[s], z_rs.at[s])

    def wait_other(k):
        row, n = ((0, 512), (512, 256), (768, 256))[k]
        whole(it.at[1, pl.ds(row, n)], c_rs.at[k])

    for s in range(4):
        arrived(s)
    whole(lq.at[0, :, 1:NX], QX_R)
    qc_copy().start()
    prepare(0)
    wait_users(0)
    wait_users(1)
    unit(0, 0)
    unit(0, 1)
    arrived(4)
    arrived(5)
    qc_copy().wait_recv()
    wait_other(0)
    prepare(1)
    prepare(3)
    for blk in (1, 3):
        unit(blk, 0)
        unit(blk, 1)
    arrived(6)
    arrived(7)
    prepare(2)
    unit(2, 0)
    unit(2, 1)
    for k in (2, 3):
        wait_users(k)
        for blk in range(4):
            unit(blk, k)
    for blk in (4, 5):
        wait_other(blk - 3)
        prepare(blk)
        for k in range(4):
            unit(blk, k)

    top = jnp.max(mst[...], axis=0)
    local = top + jnp.log2(sum(lst[k] * jnp.exp2(mst[k] - top) for k in range(NB)))
    st_out[0] = local

    def st_copy(d):
        return copy(st_out, st_in.at[(NZ - d) % NZ], ST_S, ST_R, dz=d)

    def pt_copy(d):
        return copy(pt_out.at[d], pt_in.at[(NZ - d) % NZ], PT_S, PT_R, dz=d)

    for d in (4, 3, 5, 2, 6, 1, 7):
        st_copy(d).start()

    for k in range(NB):
        lst[k] = jnp.exp2(mst[k] - local)
    for k in (3, 2, 1, 0):
        for blk in range(NB):
            weighted(blk, k)

    def part_of(s):
        return sum(acc[k, s] * lst[k, pl.ds(s, 1), :] for k in range(NB))

    def give(s, carry):
        pt_out[s] = part_of(s).astype(BF16)
        pt_copy(s).start()
        return carry

    lax.fori_loop(1, NZ, give, 0)

    whole(rows.at[1:NZ], Z_S)
    whole(it.at[0, pl.ds(0, 7 * ID)], Y_S)
    whole(lq.at[0, 1:NY, 0], QL_S)
    whole(it.at[0, pl.ds(0, 24 * ID)], X_S)
    whole(lq.at[0, :, 1:NX], QX_S)
    whole(it.at[0], C_S)
    whole(lq.at[0], QC_S)

    whole(st_in.at[1:NZ], ST_R)
    seen = [local] + [jnp.roll(st_in[e, 0], e, axis=0) for e in range(1, NZ)]
    top = functools.reduce(jnp.maximum, seen)
    lse = top + jnp.log2(sum(jnp.exp2(v - top) for v in seen))
    share = [jnp.exp2(v[0:1] - lse[0:1]) for v in seen]
    for k in range(NB):
        w = jnp.exp2(mst[k] - lse).astype(BF16)
        for i, s in enumerate(ORDER):
            w_row[k, :, i * UD : (i + 1) * UD] = w[s : s + 1, :]

    users_all = rows[...].reshape(NZ * UD, D)

    def item_part(blk, row, n):
        return dot(p_all[row : row + n, :] * w_row[blk], users_all)

    QUARTER = HALF // 2

    def xc_copy(c):
        part = pl.ds(c * QUARTER, QUARTER)
        return copy(ip.at[1, part], xc_in.at[part], XC_S, xc_rs.at[c], dc=1)

    for c, blk in ((3, 5), (2, 4), (1, 3), (0, 3)):
        part = item_part(blk, 2 * HALF + c * QUARTER, QUARTER)
        ip[1, c * QUARTER : (c + 1) * QUARTER, :] = part.astype(BF16)
        xc_copy(c).start()
    for blk in (2, 1, 0):
        own_f[spot_of(blk), :] = item_part(blk, BLOCKS[blk][1], BLOCKS[blk][2])

    def ls_copy(i, j, **to):
        ss, rs = ((L0_S, L0_R), (L1_S, L1_R), (L2_S, L2_R))[i]
        return copy(loss_out.at[i], loss_in.at[j], ss, rs, **to)

    pos_all = st_out[1] + sum(st_in[e, 1] for e in range(1, NZ))
    line = jnp.sum(jnp.sum(lse, axis=1, keepdims=True), axis=0, keepdims=True) * LN2
    loss_out[0] = jnp.broadcast_to(line, (8, 128)) - pos_all
    ls_copy(0, 0, dc=1).start()

    def xs_copy(s, e):
        return copy(
            ip.at[0, pl.ds((s * NX + e) * ID, ID)], xs_in.at[s, NX - e],
            XS_S, xs_rs.at[s], dx=e,
        )

    for c in (3, 2, 1, 0):
        xc_copy(c).wait_recv()
        if c == 3:
            whole(loss_in.at[0], L0_R)
            loss_out[1] = loss_out[0] + loss_in[0]
            for e in range(1, NX):
                ls_copy(1, e, dx=e).start()
        for k in (2 * c + 1, 2 * c):
            spot = slice(k * NX * ID, (k + 1) * NX * ID)
            total = own_f[spot, :] + xc_in[spot, :].astype(F32)
            own_f[spot, :] = total
            ip[0, spot, :] = total.astype(BF16)
            for e in (2, 1, 3):
                xs_copy(k, e).start()


    def ys_copy(s):
        mirror = SLOT[(NY - ORDER[s]) % NY]
        return copy(
            ys_out.at[s], ys_in.at[mirror], YS_S, YS_R, dy=ORDER[s]
        )

    def x_total(s):
        whole(xs_in.at[s, 1:NX], xs_rs.at[s])
        spot = slice(s * NX * ID, s * NX * ID + ID)
        return own_f[spot, :] + sum(xs_in[s, e].astype(F32) for e in range(1, NX))

    for s in range(NY - 1, 0, -1):
        ys_out[s] = x_total(s).astype(BF16)
        ys_copy(s).start()
        if s == 6:
            whole(loss_in.at[1:NX], L1_R)
            loss_out[2] = loss_out[1] + loss_in[1] + loss_in[2] + loss_in[3]
            for d in (4, 3, 5, 2, 6, 1, 7):
                ls_copy(2, 3 + d, dy=d).start()
    cand = x_total(0) - tq_s[...]

    user_sum = part_of(0) * share[0] - tv_s[...]
    whole(pt_in.at[1:NZ], PT_R)
    for e in range(1, NZ):
        user_sum = user_sum + pt_in[e].astype(F32) * share[e]
    query_ref[...] = user_sum.T * (1.0 / scaling_divisor)
    query_out = pltpu.make_async_copy(query_ref, query_hbm, out_sem.at[0])
    query_out.start()
    whole(st_in.at[1:NZ], ST_S)
    whole(pt_in.at[1:NZ], PT_S)
    whole(ip.at[1], XC_S)
    whole(xs_in.at[:, 1:NX], XS_S)
    whole(loss_in.at[0], L0_S)
    whole(loss_in.at[1:NX], L1_S)

    whole(ys_in.at[1:NY], YS_R)
    for s in range(1, NY):
        cand = cand + ys_in[s].astype(F32)
    cand_ref[...] = cand * (1.0 / scaling_divisor)
    cand_out = pltpu.make_async_copy(cand_ref, cand_hbm, out_sem.at[1])
    cand_out.start()
    total = loss_out[2]
    whole(loss_in.at[4:11], L2_R)
    for d in range(1, NY):
        total = total + loss_in[3 + d]
    loss_ref[...] = total[0:1, 0:1] * (1.0 / (2 * NX * NY * NZ * UD))
    loss_left = pltpu.make_async_copy(loss_ref, loss_hbm, out_sem.at[2])
    loss_left.start()

    whole(ys_in.at[1:NY], YS_S)
    whole(loss_in.at[4:11], L2_S)
    query_out.wait()
    cand_out.wait()
    loss_left.wait()


def settle(
    loss_in, query_in, cand_in, loss_out, query_out, cand_out,
    loss_v, query_v, cand_v, in_sem, out_sem,
):
    way = (
        (query_in, query_v, query_out), (cand_in, cand_v, cand_out), (loss_in, loss_v, loss_out)
    )
    ins = [pltpu.make_async_copy(a, v, in_sem.at[k]) for k, (a, v, _) in enumerate(way)]
    outs = [pltpu.make_async_copy(v, b, out_sem.at[k]) for k, (_, v, b) in enumerate(way)]
    for move in ins:
        move.start()
    for arrival, departure in zip(ins, outs):
        arrival.wait()
        departure.start()
    for departure in outs:
        departure.wait()


def on_device(users, items, counts, target_indices):
    dma = lambda *n: pltpu.SemaphoreType.DMA(n)
    anywhere = pl.BlockSpec(memory_space=pl.ANY)
    results = (
        jax.ShapeDtypeStruct((1, 1), F32),
        jax.ShapeDtypeStruct((UD, D), F32),
        jax.ShapeDtypeStruct((ID, D), F32),
    )
    found = pl.pallas_call(
        kernel,
        out_shape=results,
        in_specs=[anywhere] * 4,
        out_specs=(anywhere,) * 3,
        scratch_shapes=[
            pltpu.VMEM((1, 1), F32),
            pltpu.VMEM((UD, D), F32),
            pltpu.VMEM((ID, D), F32),
            pltpu.VMEM((UD, D), F32),
            pltpu.VMEM((ID, D), F32),
            pltpu.VMEM((1, ID), jnp.int32),
            pltpu.VMEM((1, UD), jnp.int32),
            dma(4),
            pltpu.VMEM((NZ, UD, D), BF16),
            pltpu.VMEM((2, 2 * HALF, D), BF16),
            pltpu.VMEM((2, NY, NX, 1, 128), F32),
            pltpu.VMEM((D, 4 * HALF), BF16),
            pltpu.VMEM((4 * HALF, 128), F32),
            pltpu.VMEM((4 * HALF, NZ * UD), BF16),
            pltpu.VMEM((NB, NZ, D, UD), F32),
            pltpu.VMEM((NB, NZ, UD), F32),
            pltpu.VMEM((NB, NZ, UD), F32),
            pltpu.VMEM((2, 8, 128), F32),
            pltpu.VMEM((NZ, 2, 8, 128), F32),
            pltpu.VMEM((NZ, D, UD), BF16),
            pltpu.VMEM((NZ, D, UD), BF16),
            pltpu.VMEM((NB, 1, NZ * UD), BF16),
            pltpu.VMEM((2 * HALF, D), F32),
            pltpu.VMEM((2, 2 * HALF, D), BF16),
            pltpu.VMEM((2 * HALF, D), BF16),
            pltpu.VMEM((NY, NX, ID, D), BF16),
            pltpu.VMEM((NY, ID, D), BF16),
            pltpu.VMEM((NY, ID, D), BF16),
            pltpu.VMEM((3, 8, 128), F32),
            pltpu.VMEM((11, 8, 128), F32),
            pltpu.VMEM((ID, D), F32),
            pltpu.VMEM((D, UD), F32),
            dma(15), dma(NZ), dma(NY), dma(NY), dma(3), dma(4), dma(NY), dma(9), dma(3),
        ],
        compiler_params=pltpu.CompilerParams(
            collective_id=0, has_side_effects=True, vmem_limit_bytes=64 * 2**20
        ),
        cost_estimate=pl.CostEstimate(
            flops=6 * 1024 * 2048 * D, bytes_accessed=2**19, transcendentals=1024 * 2048
        ),
        name="towers",
    )(users, items, counts.reshape(1, ID), target_indices.reshape(1, UD))
    loss, query, cand = pl.pallas_call(
        settle,
        out_shape=results,
        in_specs=[anywhere] * 3,
        out_specs=(anywhere,) * 3,
        scratch_shapes=[
            pltpu.VMEM((1, 1), F32), pltpu.VMEM((UD, D), F32), pltpu.VMEM((ID, D), F32), dma(3), dma(3)
        ],
        compiler_params=pltpu.CompilerParams(vmem_limit_bytes=64 * 2**20),
        name="settle",
    )(*found)
    return loss.reshape(()), query, cand


def solution(mesh):
    placed = P(("blk", "grp"))
    wide = P(("blk", "grp"), None)
    return jax.shard_map(
        on_device,
        mesh=mesh,
        in_specs=(wide, wide, placed, placed),
        out_specs=(P(), wide, wide),
        check_vma=False,
    )
```
